32 devices in a mesh: rve: 8 (over z, y), blk: 4 (over x, core).
Axes of the slice: x: 2, y: 2, z: 4, core: 2. Of those that a mesh axis runs over, the one named last changes fastest.
Arguments:
- strain: bfloat16 [864, 6], P(('rve', 'blk')), may hold values from -6 to 6
- fiber_coeff: bfloat16 [864, 2048], P(('rve', 'blk')), may hold values from 0.049804688 to 0.8984375
- gradients: float32 [12, 864], P(None, ('rve', 'blk')), may hold values from -6 to 6
- volume: float32 [864], P(('rve', 'blk')), may hold values from 0.1 to 1
- corners: int32 [4, 864], P(None, ('rve', 'blk')), may hold values from 0 to 4095, as said below
- rve_worker: int32 [864], P(('rve', 'blk')), may hold values from 0 to 7, as said below
- rve_slot: int32 [864], P(('rve', 'blk')), may hold values from 0 to 80, as said below
- slot_element: int32 [2592], P(('rve', 'blk')), may hold values from -1 to 863, as said below
- state_table: float32 [2592, 3, 2048], P(('rve', 'blk')), may hold values from -6 to 6
- loading: bfloat16 [6, 3, 2048], replicated, may hold values from -6 to 6
- compliance: bfloat16 [2048, 2048], P('rve'), as said below
Outputs:
- new_states: float32 [2592, 3, 2048], P(('rve', 'blk'))
- node_forces: float32 [3, 4096], P(None, ('rve', 'blk'))
- node_blocks: float32 [9, 4096], P(None, ('rve', 'blk'))
The draws below stay inside these ranges and needn't reach their ends.
Inputs may be any that keep to these rules, and one draw needn't show every extreme that they name: `rve_worker`: counting the elements of one blk index, each worker number holds between 9 and 81 RVEs, the most reached by some worker; the elements of one aligned block of 27 that name one worker number are never more than 11, a count reached in every draw. `rve_slot`: A worker's RVEs fill its slots from 0 upward; no two elements share a worker and slot. `slot_element`: entry (w * 4 + b) * 81 + s holds e exactly when rve_worker[e] = w, (e // 27) % 4 = b and rve_slot[e] = s; every other entry is -1. The corners of elements in aligned block k of 27 elements are nodes k * 128 to (k + 2) * 128 - 1, and in the last block nodes k * 128 to (k + 1) * 128 - 1. `compliance`: Symmetric.
All inputs are finite; a program needn't handle non-finite values.
Results may differ from the reference program's by a relative error of at most 0.0023.
Values may be sent and summed in bfloat16 or wider, within the bound.
A program may use at most 64 MiB of HBM per device.

```python
import math
import jax
import jax.numpy as jnp
import numpy as np
from jax import lax

NODES = 2048
ITERS = 3
ELEM_DEV = 27
NODE_DEV = 128
CAP = 81
ELEMS = 864
NODES_ALL = 4096
N_RVE = 8
N_BLK = 4


def column_assignment(key, column):
    top_step = 2 * ELEM_DEV // 3
    key_order, key_steps = jax.random.split(jax.random.fold_in(jax.random.fold_in(key, 17), column))
    step_sizes = jax.random.randint(key_steps, ((N_RVE + 3) // 4,), 0, top_step + 1)
    step_sizes = step_sizes.at[0].set(top_step)
    position = jnp.arange(N_RVE)
    grouped = step_sizes[position // 4]
    lead = (position % 4 == 0) & (position + 3 < N_RVE)
    follow = (position % 4 != 0) & (position - position % 4 + 3 < N_RVE)
    by_position = jnp.where(lead, ELEM_DEV + 3 * grouped, jnp.where(follow, ELEM_DEV - grouped, ELEM_DEV))
    worker_loads = by_position[jax.random.permutation(key_order, N_RVE)]
    range_ends = jnp.cumsum(worker_loads)
    range_starts = range_ends - worker_loads
    return (worker_loads, range_starts, range_ends)


def assignment(key):
    return jax.vmap(lambda column: column_assignment(key, column))(jnp.arange(N_BLK))


def element_worker(key):
    worker_loads, range_starts, range_ends = assignment(key)
    element = jnp.arange(ELEMS)
    device = element // ELEM_DEV
    column = device % N_BLK
    row_index = device // N_BLK
    global_rank = element % ELEM_DEV * N_RVE + row_index
    chosen = jnp.sum(range_ends[column] <= global_rank[:, None], axis=1)
    return (chosen, global_rank - range_starts[column, chosen])


def draw_rve_worker(key, part):
    chosen, slots = element_worker(key)
    return chosen.astype(jnp.int32)


def draw_rve_slot(key, part):
    chosen, slots = element_worker(key)
    return slots.astype(jnp.int32)


def draw_slot_element(key, part):
    worker_loads, range_starts, range_ends = assignment(key)
    slot_index = jnp.arange(N_RVE * N_BLK * CAP)
    device = slot_index // CAP
    within = slot_index % CAP
    column = device % N_BLK
    owner_worker = device // N_BLK
    global_rank = range_starts[column, owner_worker] + within
    element = (global_rank % N_RVE * N_BLK + column) * ELEM_DEV + global_rank // N_RVE
    return jnp.where(within < worker_loads[column, owner_worker], element, -1).astype(jnp.int32)


def draw_corners(key, part):
    blocks_all = ELEMS // ELEM_DEV
    element = jnp.arange(ELEMS)
    home_block = element // ELEM_DEV
    reach = jnp.where(home_block == blocks_all - 1, NODE_DEV, 2 * NODE_DEV)
    offsets = jax.random.randint(jax.random.fold_in(key, 29), (4, ELEMS), 0, 2 * NODE_DEV) % reach[None, :]
    corner_row = jnp.arange(4)[:, None]
    offsets = jnp.where((corner_row == 0) & (element % ELEM_DEV == 0)[None, :], 0, offsets)
    offsets = jnp.where((corner_row == 3) & (element % ELEM_DEV == ELEM_DEV - 1)[None, :], reach[None, :] - 1, offsets)
    return (home_block[None, :] * NODE_DEV + offsets).astype(jnp.int32)


def draw_compliance(key, part):
    noise_key = jax.random.fold_in(key, 41)
    random_part = jax.random.normal(noise_key, (NODES, NODES), jnp.float32)
    symmetric = (random_part + random_part.T) * (0.3 / math.sqrt(2.0 * NODES))
    return (symmetric + jnp.eye(NODES, dtype=jnp.float32)).astype(jnp.bfloat16)


def shard_levels(stream_key, dims, cuts, low, high):
    def one(axis_at, blocks):
        heights = jax.random.uniform(jax.random.fold_in(jax.random.fold_in(stream_key, 6), axis_at), (blocks,), jnp.float32, low / len(cuts), high / len(cuts))
        return jnp.repeat(jnp.exp(heights), dims[axis_at] // blocks).reshape((-1,) + (1,) * (len(dims) - axis_at - 1))

    loudness = one(*cuts[0])
    for cut in cuts[1:]:
        loudness = loudness * one(*cut)
    return loudness


def centred(key, shape, width, limit, cuts=(), kind=jnp.bfloat16):
    result = jax.random.normal(key, shape, jnp.float32) * width
    if len(cuts) > 0:
        result = shard_levels(key, shape, cuts, -0.22, 0.18) * result
    return jnp.clip(result, min=-limit, max=limit).astype(kind)


def setup_inputs(seed: int = 0) -> dict:
    key_of = jax.random.split(jax.random.key(seed), 12)
    return {
        "strain": centred(key_of[0], (ELEMS, 6), 0.4, 6.0, ((0, 32),)),
        "fiber_coeff": jnp.clip(jnp.exp(math.log(0.8984375) - 2.892548 * jax.random.uniform(key_of[1], (ELEMS, NODES), jnp.float32) ** shard_levels(key_of[1], (ELEMS, NODES), ((0, 32),), -0.2, 0.2)), 0.049804688, 0.8984375).astype(jnp.bfloat16),
        "gradients": centred(key_of[2], (12, ELEMS), 1.0, 6.0, ((1, 32),), jnp.float32),
        "volume": jnp.clip(jnp.exp(math.log(1.0) - 2.3025851 * jax.random.uniform(key_of[3], (ELEMS,), jnp.float32) ** shard_levels(key_of[3], (ELEMS,), ((0, 32),), -0.2, 0.2)), 0.1, 1.0),
        "corners": draw_corners(jax.random.fold_in(key_of[11], 71), 0),
        "rve_worker": draw_rve_worker(jax.random.fold_in(key_of[11], 71), 0),
        "rve_slot": draw_rve_slot(jax.random.fold_in(key_of[11], 71), 0),
        "slot_element": draw_slot_element(jax.random.fold_in(key_of[11], 71), 0),
        "state_table": centred(key_of[8], (N_RVE * N_BLK * CAP, 3, NODES), 0.5, 6.0, ((0, 32),), jnp.float32),
        "loading": centred(key_of[9], (6, 3, NODES), 1.0, 6.0),
        "compliance": draw_compliance(jax.random.fold_in(key_of[11], 71), 0),
    }


highest = lax.Precision.HIGHEST


def strain_map():
    voigt_map = np.zeros((6, 3, 3), np.float32)
    for voigt_row, first_axis, second_axis in ((0, 0, 0), (1, 1, 1), (2, 2, 2), (3, 1, 2), (3, 2, 1), (4, 0, 2), (4, 2, 0), (5, 0, 1), (5, 1, 0)):
        voigt_map[voigt_row, first_axis, second_axis] = 1.0
    return jnp.asarray(voigt_map)


def micro_block(inputs, loading, compliance):
    strain_rows, coeff_rows, start_rows = inputs
    batch_rows = strain_rows.shape[0]
    forcing = jnp.dot(strain_rows, loading.reshape(6, 3 * NODES), preferred_element_type=jnp.float32).reshape(batch_rows, 3, NODES)
    current = start_rows
    for iteration in range(ITERS):
        pressure = (forcing - coeff_rows.astype(jnp.float32)[:, None, :] * jnp.tanh(current)).astype(jnp.bfloat16)
        current = jnp.dot(pressure.reshape(batch_rows * 3, NODES), compliance.T, preferred_element_type=jnp.float32).reshape(batch_rows, 3, NODES)
    return current


def reference(strain, fiber_coeff, gradients, volume, corners, rve_worker, rve_slot, slot_element, state_table, loading, compliance):
    blocks_all = ELEMS // ELEM_DEV
    column = ((jnp.arange(ELEMS) // ELEM_DEV) % N_BLK).astype(jnp.int32)
    flat_index = ((rve_worker * N_BLK + column) * CAP + rve_slot).astype(jnp.int32)
    starting = state_table[flat_index]
    blocks = (strain.reshape(blocks_all, ELEM_DEV, 6), fiber_coeff.reshape(blocks_all, ELEM_DEV, NODES), starting.reshape(blocks_all, ELEM_DEV, 3, NODES))
    finals = lax.map(lambda inputs: micro_block(inputs, loading, compliance), blocks).reshape(ELEMS, 3, NODES)
    occupied = slot_element >= 0
    picked = finals[jnp.maximum(slot_element, 0).astype(jnp.int32)]
    new_states = jnp.where(occupied[:, None, None], picked, state_table)
    mean_scale = 1.0 / (3 * NODES)
    load_float = loading.reshape(6, 3 * NODES).astype(jnp.float32)
    basis = jnp.dot(loading.reshape(18, NODES), compliance.T, preferred_element_type=jnp.float32).reshape(6, 3 * NODES)
    flat_state = finals.reshape(ELEMS, 3 * NODES)
    stress = jnp.dot(flat_state, load_float.T, precision=highest) * mean_scale
    fixed_part = jnp.dot(load_float, basis.T, precision=highest)
    products = (basis[:, None, :] * basis[None, :, :]).reshape(36, 3 * NODES)
    damping = (fiber_coeff.astype(jnp.float32)[:, None, :] * (1.0 - jnp.tanh(finals) ** 2)).reshape(ELEMS, 3 * NODES)
    tangent = (fixed_part.reshape(1, 36) - jnp.dot(damping, products.T, precision=highest)) * mean_scale
    gradient_rows = gradients.reshape(4, 3, ELEMS)
    bmatrix = jnp.einsum("vac,ich->ivah", strain_map(), gradient_rows, precision=highest)
    corner_force = volume * jnp.einsum("ivah,hv->iah", bmatrix, stress, precision=highest)
    corner_block = volume * jnp.einsum("ivah,hvw,iwbh->iabh", bmatrix, tangent.reshape(ELEMS, 6, 6), bmatrix, precision=highest)
    contrib = jnp.concatenate([corner_force, corner_block.reshape(4, 9, ELEMS)], axis=1)
    values = jnp.transpose(contrib, (0, 2, 1)).reshape(4 * ELEMS, 12)
    assembled = jax.ops.segment_sum(values, corners.reshape(4 * ELEMS).astype(jnp.int32), num_segments=NODES_ALL)
    return new_states, assembled[:, :3].T, assembled[:, 3:].T
```

```python
import jax
import jax.numpy as jnp
import numpy as np
from jax import lax
from jax.experimental import pallas as pl
from jax.experimental.pallas import tpu as pltpu
from jax.sharding import PartitionSpec as P

ITERS = 3
NODE_DEV = 128


highest = lax.Precision.HIGHEST


def from_behind(block, axis, distance):
    devices = range(lax.axis_size(axis))
    route = [(i - distance, i) for i in devices if i - distance in devices]
    return lax.ppermute(block, axis, route)


def strain_map():
    voigt_map = np.zeros((6, 3, 3), np.float32)
    for voigt_row, first_axis, second_axis in (
        (0, 0, 0),
        (1, 1, 1),
        (2, 2, 2),
        (3, 1, 2),
        (3, 2, 1),
        (4, 0, 2),
        (4, 2, 0),
        (5, 0, 1),
        (5, 1, 0),
    ):
        voigt_map[voigt_row, first_axis, second_axis] = 1.0
    return jnp.asarray(voigt_map)


def micro_solve(strain_rows, coeff_rows, start_rows, loading, network, basis, fixed_part):
    batch_rows = strain_rows.shape[0]
    node_count = network.shape[0]
    mean_scale = 1.0 / (3 * node_count)
    forcing = jnp.dot(
        strain_rows, loading.reshape(6, 3 * node_count), preferred_element_type=jnp.float32
    ).reshape(batch_rows, 3, node_count)
    fiber_wide = coeff_rows[:, None, :].astype(jnp.float32)
    current = start_rows.reshape(batch_rows, 3, node_count)
    for iteration in range(ITERS):
        pressure = (
            (forcing - fiber_wide * jnp.tanh(current))
            .astype(jnp.bfloat16)
            .reshape(batch_rows * 3, node_count)
        )
        current = lax.dot_general(
            pressure, network, (((1,), (1,)), ((), ())), preferred_element_type=jnp.float32
        ).reshape(batch_rows, 3, node_count)
    flat_state = current.reshape(batch_rows, 3 * node_count)
    load_float = loading.reshape(6, 3 * node_count).astype(jnp.float32)
    stress = jnp.dot(flat_state, load_float.T, precision=highest) * mean_scale
    products = (basis[:, None, :] * basis[None, :, :]).reshape(36, 3 * node_count)
    damping = (fiber_wide * (1.0 - jnp.tanh(current) ** 2)).reshape(batch_rows, 3 * node_count)
    tangent = (
        fixed_part.reshape(1, 36) - jnp.dot(damping, products.T, precision=highest)
    ) * mean_scale
    return (flat_state, stress, tangent)


def body(
    strain,
    fiber_coeff,
    gradients,
    volume,
    corners,
    rve_worker,
    rve_slot,
    slot_element,
    state_table,
    loading,
    compliance,
):
    elem_rows = strain.shape[0]
    workers = lax.axis_size("rve")
    columns = lax.axis_size("blk")
    capacity = state_table.shape[0]
    slot_cap = (capacity + workers - 1) // workers
    node_count = compliance.shape[1]
    buffer_rows = workers * slot_cap
    network = lax.all_gather(compliance, "rve", axis=0, tiled=True)
    basis = lax.dot_general(
        loading.reshape(18, node_count),
        network,
        (((1,), (1,)), ((), ())),
        preferred_element_type=jnp.float32,
    ).reshape(6, 3 * node_count)
    fixed_part = jnp.dot(
        loading.reshape(6, 3 * node_count).astype(jnp.float32), basis.T, precision=highest
    )
    earlier = (rve_worker[None, :] == rve_worker[:, None]) & (rve_slot[None, :] < rve_slot[:, None])
    home_pos = rve_worker * slot_cap + jnp.sum(earlier, axis=1)
    occupied = slot_element >= 0
    source_home = jnp.where(occupied, slot_element // elem_rows // columns, -1)
    slot_ids = jnp.arange(capacity)
    before = (source_home[None, :] == source_home[:, None]) & (
        slot_ids[None, :] < slot_ids[:, None]
    )
    work_pos = jnp.where(occupied, source_home * slot_cap + jnp.sum(before, axis=1), buffer_rows)
    fetch_pos = jnp.minimum(work_pos, buffer_rows - 1)
    flat_table = state_table.reshape(capacity, 3 * node_count)
    send_strain = jnp.zeros((buffer_rows, 6), jnp.bfloat16).at[home_pos].set(strain)
    send_coeff = jnp.zeros((buffer_rows, node_count), jnp.bfloat16).at[home_pos].set(fiber_coeff)
    got_strain, got_coeff = (
        lax.all_to_all(
            send_strain.reshape(workers, slot_cap, 6),
            "rve",
            split_axis=0,
            concat_axis=0,
            tiled=True,
        ),
        lax.all_to_all(
            send_coeff.reshape(workers, slot_cap, node_count),
            "rve",
            split_axis=0,
            concat_axis=0,
            tiled=True,
        ),
    )
    slot_strain = jnp.where(occupied[:, None], got_strain.reshape(buffer_rows, 6)[fetch_pos], 0)
    slot_coeff = jnp.where(
        occupied[:, None], got_coeff.reshape(buffer_rows, node_count)[fetch_pos], 0
    )
    finals, slot_stress, slot_tangent = micro_solve(
        slot_strain, slot_coeff, flat_table, loading, network, basis, fixed_part
    )
    new_table = jnp.where(occupied[:, None], finals, flat_table)
    back_stress = (
        jnp.zeros((buffer_rows, 6), jnp.float32).at[work_pos].set(slot_stress, mode="drop")
    )
    back_tangent = (
        jnp.zeros((buffer_rows, 36), jnp.float32).at[work_pos].set(slot_tangent, mode="drop")
    )
    ret_stress, ret_tangent = (
        lax.all_to_all(
            back_stress.reshape(workers, slot_cap, 6),
            "rve",
            split_axis=0,
            concat_axis=0,
            tiled=True,
        ),
        lax.all_to_all(
            back_tangent.reshape(workers, slot_cap, 36),
            "rve",
            split_axis=0,
            concat_axis=0,
            tiled=True,
        ),
    )
    stress = ret_stress.reshape(buffer_rows, 6)[home_pos]
    tangent = ret_tangent.reshape(buffer_rows, 36)[home_pos]
    gradient_rows = gradients.reshape(4, 3, elem_rows)
    bmatrix = jnp.einsum("vac,ich->ivah", strain_map(), gradient_rows, precision=highest)
    corner_force = volume * jnp.einsum("ivah,hv->iah", bmatrix, stress, precision=highest)
    corner_block = volume * jnp.einsum(
        "ivah,hvw,iwbh->iabh", bmatrix, tangent.reshape(elem_rows, 6, 6), bmatrix, precision=highest
    )
    contrib = jnp.concatenate([corner_force, corner_block.reshape(4, 9, elem_rows)], axis=1)
    contrib = jnp.transpose(contrib, (1, 0, 2)).reshape(12, 4 * elem_rows)
    device_rank = lax.axis_index("rve") * columns + lax.axis_index("blk")
    local_node = (corners - device_rank * NODE_DEV).reshape(4 * elem_rows)
    onehot = (local_node[:, None] == jnp.arange(2 * NODE_DEV)[None, :]).astype(jnp.float32)
    assembled = jnp.dot(contrib, onehot, precision=highest)
    own_rows = assembled[:, :NODE_DEV] + from_behind(assembled[:, NODE_DEV:], ("rve", "blk"), 1)
    return (new_table.reshape(capacity, 3, node_count), own_rows[:3], own_rows[3:])


ROW = 16
SLOT_PAD = 88
LOAD_PAD = 24


def to_column(row):
    count = row.shape[1]
    grid_row = lax.broadcasted_iota(jnp.int32, (count, count), 0)
    grid_col = lax.broadcasted_iota(jnp.int32, (count, count), 1)
    return jnp.sum(jnp.where(grid_row == grid_col, row, 0), axis=1, keepdims=True)


def home_positions(worker_row, slot_row):
    same = to_column(worker_row) == worker_row
    ahead = to_column(slot_row) < slot_row
    rank = jnp.sum(jnp.where(same & ahead, 1, 0), axis=0, keepdims=True)
    return worker_row * ROW + rank


def home_onehot(worker_row, slot_row, rows):
    positions = home_positions(worker_row, slot_row)
    row_ids = lax.broadcasted_iota(jnp.int32, (rows, positions.shape[1]), 0)
    return (row_ids == positions).astype(jnp.float32)


def work_onehot(source_row, rows):
    count = source_row.shape[1]
    slot_ids = lax.broadcasted_iota(jnp.int32, (count, count), 0)
    later_ids = lax.broadcasted_iota(jnp.int32, (count, count), 1)
    same = to_column(source_row) == source_row
    rank = jnp.sum(jnp.where(same & (slot_ids < later_ids), 1, 0), axis=0, keepdims=True)
    positions = jnp.where(source_row >= 0, source_row * ROW + rank, -1)
    column = to_column(positions)
    lanes = lax.broadcasted_iota(jnp.int32, (count, rows), 1)
    return (lanes == column).astype(jnp.float32)


def dot_nt(left, right, **kwargs):
    return lax.dot_general(
        left, right, (((1,), (1,)), ((), ())), preferred_element_type=jnp.float32, **kwargs
    )


def dot_tn(left, right, **kwargs):
    return lax.dot_general(
        left, right, (((0,), (0,)), ((), ())), preferred_element_type=jnp.float32, **kwargs
    )


def split_wide(values):
    high = values.astype(jnp.bfloat16)
    return high, (values - high.astype(jnp.float32)).astype(jnp.bfloat16)


def pack_kernel(strain_ref, fiber_ref, worker_ref, slot_ref, send_ref):
    rows = send_ref.shape[0]
    nodes = fiber_ref.shape[1]
    onehot = home_onehot(worker_ref[...], slot_ref[...], rows).astype(jnp.bfloat16)
    send_ref[:, :nodes] = jnp.dot(
        onehot, fiber_ref[...], preferred_element_type=jnp.float32
    ).astype(jnp.bfloat16)
    send_ref[:, nodes:] = dot_nt(onehot, strain_ref[...]).astype(jnp.bfloat16)


def micro_kernel(
    got_ref, source_ref, state_ref, loading_ref, halves_ref, new_ref, back_ref,
    dense, forcing, coeff, current, pressure_a, pressure_b
):
    workers, block = halves_ref.shape[0], halves_ref.shape[1]
    nodes = state_ref.shape[2]
    capacity = state_ref.shape[1]
    rows = got_ref.shape[0]
    mean_scale = 1.0 / (3 * nodes)
    near = workers // 2
    for owner in range(workers):
        for step in range(near + 1):
            other = (owner + step) % workers
            if step == near and owner >= near:
                continue
            tile = halves_ref[owner, :, step * block:(step + 1) * block]
            dense[owner * block:(owner + 1) * block, other * block:(other + 1) * block] = tile
            if step:
                dense[other * block:(other + 1) * block, owner * block:(owner + 1) * block] = tile.T
    onehot = work_onehot(source_ref[...], rows)
    onehot = jnp.concatenate(
        [onehot, jnp.zeros((SLOT_PAD - capacity, rows), jnp.float32)], axis=0
    )
    fetch = onehot.astype(jnp.bfloat16)
    slots = jnp.dot(fetch, got_ref[...], preferred_element_type=jnp.float32)
    coeff[...] = slots[:, :nodes]
    strain_rows = slots[:, nodes:nodes + 8].astype(jnp.bfloat16)
    forcing[0:LOAD_PAD, :] = loading_ref[...].astype(jnp.float32)
    current[0:LOAD_PAD, :] = jnp.zeros((LOAD_PAD, nodes), jnp.float32)
    for axis in range(3):
        start = LOAD_PAD + axis * SLOT_PAD
        load = forcing[axis * 8:axis * 8 + 8, :].astype(jnp.bfloat16)
        forcing[start:start + SLOT_PAD, :] = jnp.dot(
            strain_rows, load, preferred_element_type=jnp.float32
        )
        current[start + 80:start + SLOT_PAD, :] = jnp.zeros((SLOT_PAD - 80, nodes), jnp.float32)
        current[start:start + capacity, :] = state_ref[axis]

    def press(values, lanes):
        c = coeff[:, lanes]
        wide = jnp.concatenate([jnp.zeros((LOAD_PAD, c.shape[1]), jnp.float32), c, c, c], axis=0)
        return (forcing[:, lanes] - wide * jnp.tanh(values)).astype(jnp.bfloat16)

    for tile in range(nodes // block):
        lanes = slice(tile * block, (tile + 1) * block)
        pressure_a[:, lanes] = press(current[:, lanes], lanes)
    for iteration in range(ITERS):
        reads, writes = (pressure_a, pressure_b) if iteration % 2 == 0 else (pressure_b, pressure_a)
        for tile in range(nodes // block):
            lanes = slice(tile * block, (tile + 1) * block)
            values = jnp.dot(reads[...], dense[:, lanes], preferred_element_type=jnp.float32)
            if iteration == ITERS - 1:
                current[:, lanes] = values
            else:
                writes[:, lanes] = press(values, lanes)

    occupied = jnp.sum(onehot, axis=1, keepdims=True) > 0.5
    tangent = jnp.zeros((SLOT_PAD, 96), jnp.float32)
    tangent_low = jnp.zeros((SLOT_PAD, 48), jnp.float32)
    stress = jnp.zeros((SLOT_PAD, 8), jnp.float32)
    fixed = jnp.zeros((8, 8), jnp.float32)
    for axis in range(3):
        start = LOAD_PAD + axis * SLOT_PAD
        final = current[start:start + SLOT_PAD, :]
        new_ref[axis] = jnp.where(
            occupied[:capacity], current[start:start + capacity, :], state_ref[axis]
        )
        basis = current[axis * 8:axis * 8 + 8, :]
        load = forcing[axis * 8:axis * 8 + 8, :].astype(jnp.bfloat16)
        products = jnp.concatenate([basis[k:k + 1, :] * basis for k in range(6)], axis=0)
        products_high, products_low = split_wide(products)
        damping = coeff[...] * (1.0 - jnp.tanh(final) ** 2)
        damping_high, damping_low = split_wide(damping)
        tangent += dot_nt(damping_high, jnp.concatenate([products_high, products_low], axis=0))
        tangent_low += dot_nt(damping_low, products_high)
        final_high, final_low = split_wide(final)
        stress += dot_nt(final_high, load) + dot_nt(final_low, load)
        basis_high, basis_low = split_wide(basis)
        fixed += dot_nt(load, basis_high) + dot_nt(load, basis_low)
    lane_ids = lax.broadcasted_iota(jnp.int32, (8, 48), 1)
    row_ids = lax.broadcasted_iota(jnp.int32, (8, 48), 0)
    spread = jnp.dot(
        fixed, (lane_ids % 8 == row_ids).astype(jnp.float32), precision=highest,
        preferred_element_type=jnp.float32,
    )
    fixed_row = jnp.sum(jnp.where(lane_ids // 8 == row_ids, spread, 0.0), axis=0, keepdims=True)
    total = fixed_row - (tangent[:, :48] + tangent[:, 48:] + tangent_low)
    packed = jnp.concatenate(
        [total, stress, jnp.zeros((SLOT_PAD, 72), jnp.float32)], axis=1
    ) * mean_scale
    back_ref[...] = dot_tn(onehot, packed, precision=highest)


def assemble_kernel(ret_ref, worker_ref, slot_ref, gradient_ref, volume_ref, corner_ref, own_ref, next_ref):
    rows = ret_ref.shape[0]
    onehot = home_onehot(worker_ref[...], slot_ref[...], rows)
    values = dot_tn(ret_ref[...], onehot, precision=highest)
    volume = volume_ref[...]
    count = volume.shape[1]
    stress = [values[48 + k:49 + k, :] for k in range(6)]
    rows_of = [values[k * 8:k * 8 + 8, :] for k in range(6)]
    node_ids = lax.broadcasted_iota(jnp.int32, (2 * NODE_DEV, count), 0)
    assembled = jnp.zeros((16, 2 * NODE_DEV), jnp.float32)

    def apply(g, terms):
        gx, gy, gz = g
        return (
            gx * terms[0] + gz * terms[4] + gy * terms[5],
            gy * terms[1] + gz * terms[3] + gx * terms[5],
            gz * terms[2] + gy * terms[3] + gx * terms[4],
        )

    for corner in range(4):
        g = [gradient_ref[3 * corner + c:3 * corner + c + 1, :] for c in range(3)]
        lines = [volume * f for f in apply(g, stress)]
        for u in apply(g, rows_of):
            lines += [volume * m for m in apply(g, [u[j:j + 1, :] for j in range(6)])]
        contrib = jnp.concatenate(lines + [jnp.zeros((4, count), jnp.float32)], axis=0)
        picked = (node_ids == corner_ref[corner:corner + 1, :]).astype(jnp.float32)
        assembled += dot_nt(contrib, picked, precision=highest)
    own_ref[...] = assembled[:, :NODE_DEV]
    next_ref[...] = assembled[:, NODE_DEV:]


def half_network(compliance, workers, columns):
    block, nodes = compliance.shape
    mine = lax.axis_index("rve")
    part = block // columns
    rows = lax.dynamic_slice(compliance, (lax.axis_index("blk") * part, 0), (part, nodes))
    doubled = jnp.concatenate([rows, rows], axis=1)
    near = workers // 2
    half = lax.dynamic_slice(doubled, (0, mine * block), (part, (near + 1) * block))
    gathered = lax.all_gather(half, ("rve", "blk"), axis=0, tiled=True)
    return gathered.reshape(workers, block, (near + 1) * block)


def tiled_body(
    strain, fiber_coeff, gradients, volume, corners, rve_worker, rve_slot, slot_element,
    state_table, loading, compliance,
):
    elem_rows = strain.shape[0]
    workers = lax.axis_size("rve")
    columns = lax.axis_size("blk")
    capacity = state_table.shape[0]
    nodes = compliance.shape[1]
    block = compliance.shape[0]
    rows = workers * ROW
    vmem = pl.BlockSpec(memory_space=pltpu.VMEM)
    params = pltpu.CompilerParams(vmem_limit_bytes=56 * 2**20)
    halves = half_network(compliance, workers, columns)
    worker_row, slot_row = rve_worker[None, :], rve_slot[None, :]
    strain_lanes = jnp.pad(strain.T, ((0, 122), (0, 0)))
    send = pl.pallas_call(
        pack_kernel,
        out_shape=jax.ShapeDtypeStruct((rows, nodes + 128), jnp.bfloat16),
        in_specs=[vmem] * 4, out_specs=vmem, compiler_params=params, name="pack",
    )(strain_lanes, fiber_coeff, worker_row, slot_row)
    got = lax.all_to_all(
        send.reshape(workers, ROW, nodes + 128), "rve", split_axis=0, concat_axis=0, tiled=True
    ).reshape(rows, nodes + 128)
    source = jnp.where(slot_element >= 0, slot_element // (elem_rows * columns), -1)[None, :]
    load_rows = jnp.pad(jnp.transpose(loading, (1, 0, 2)), ((0, 0), (0, 2), (0, 0)))
    load_rows = load_rows.reshape(LOAD_PAD, nodes)
    total_rows = LOAD_PAD + 3 * SLOT_PAD
    new_table, back = pl.pallas_call(
        micro_kernel,
        out_shape=(
            jax.ShapeDtypeStruct((3, capacity, nodes), jnp.float32),
            jax.ShapeDtypeStruct((rows, 128), jnp.float32),
        ),
        in_specs=[vmem] * 5, out_specs=(vmem, vmem),
        scratch_shapes=[
            pltpu.VMEM((nodes, nodes), jnp.bfloat16),
            pltpu.VMEM((total_rows, nodes), jnp.float32),
            pltpu.VMEM((SLOT_PAD, nodes), jnp.float32),
            pltpu.VMEM((total_rows, nodes), jnp.float32),
            pltpu.VMEM((total_rows, nodes), jnp.bfloat16),
            pltpu.VMEM((total_rows, nodes), jnp.bfloat16),
        ],
        compiler_params=params, name="micro",
    )(got, source, jnp.transpose(state_table, (1, 0, 2)), load_rows, halves)
    ret = lax.all_to_all(
        back.reshape(workers, ROW, 128), "rve", split_axis=0, concat_axis=0, tiled=True
    ).reshape(rows, 128)
    device_rank = lax.axis_index("rve") * columns + lax.axis_index("blk")
    own, following = pl.pallas_call(
        assemble_kernel,
        out_shape=(jax.ShapeDtypeStruct((16, NODE_DEV), jnp.float32),) * 2,
        in_specs=[vmem] * 6, out_specs=(vmem, vmem), compiler_params=params, name="assemble",
    )(ret, worker_row, slot_row, gradients, volume[None, :], corners - device_rank * NODE_DEV)
    own_rows = own + from_behind(following, ("rve", "blk"), 1)
    return jnp.transpose(new_table, (1, 0, 2)), own_rows[:3], own_rows[3:12]


def solution(mesh):
    def chosen(*args):
        workers, columns = lax.axis_size("rve"), lax.axis_size("blk")
        block = args[-1].shape[0]
        even = workers % 2 == 0 and block % 128 == 0 and block % (16 * columns) == 0
        few = -(-args[8].shape[0] // workers) <= ROW and args[8].shape[0] <= SLOT_PAD
        return (tiled_body if even and few else body)(*args)

    return jax.shard_map(
        chosen,
        mesh=mesh,
        in_specs=(
            P(("rve", "blk"), None),
            P(("rve", "blk"), None),
            P(None, ("rve", "blk")),
            P(("rve", "blk")),
            P(None, ("rve", "blk")),
            P(("rve", "blk")),
            P(("rve", "blk")),
            P(("rve", "blk")),
            P(("rve", "blk"), None, None),
            P(),
            P("rve", None),
        ),
        out_specs=(P(("rve", "blk"), None, None), P(None, ("rve", "blk")), P(None, ("rve", "blk"))),
        check_vma=False,
    )
```

```python
import jax
import jax.numpy as jnp
import numpy as np
from jax import lax
from jax.experimental import pallas as pl
from jax.experimental.pallas import tpu as pltpu
from jax.sharding import PartitionSpec as P

ITERS = 3
NODE_DEV = 128


highest = lax.Precision.HIGHEST


def from_behind(block, axis, distance):
    devices = range(lax.axis_size(axis))
    route = [(i - distance, i) for i in devices if i - distance in devices]
    return lax.ppermute(block, axis, route)


def strain_map():
    voigt_map = np.zeros((6, 3, 3), np.float32)
    for voigt_row, first_axis, second_axis in (
        (0, 0, 0),
        (1, 1, 1),
        (2, 2, 2),
        (3, 1, 2),
        (3, 2, 1),
        (4, 0, 2),
        (4, 2, 0),
        (5, 0, 1),
        (5, 1, 0),
    ):
        voigt_map[voigt_row, first_axis, second_axis] = 1.0
    return jnp.asarray(voigt_map)


def micro_solve(strain_rows, coeff_rows, start_rows, loading, network, basis, fixed_part):
    batch_rows = strain_rows.shape[0]
    node_count = network.shape[0]
    mean_scale = 1.0 / (3 * node_count)
    forcing = jnp.dot(
        strain_rows, loading.reshape(6, 3 * node_count), preferred_element_type=jnp.float32
    ).reshape(batch_rows, 3, node_count)
    fiber_wide = coeff_rows[:, None, :].astype(jnp.float32)
    current = start_rows.reshape(batch_rows, 3, node_count)
    for iteration in range(ITERS):
        pressure = (
            (forcing - fiber_wide * jnp.tanh(current))
            .astype(jnp.bfloat16)
            .reshape(batch_rows * 3, node_count)
        )
        current = lax.dot_general(
            pressure, network, (((1,), (1,)), ((), ())), preferred_element_type=jnp.float32
        ).reshape(batch_rows, 3, node_count)
    flat_state = current.reshape(batch_rows, 3 * node_count)
    load_float = loading.reshape(6, 3 * node_count).astype(jnp.float32)
    stress = jnp.dot(flat_state, load_float.T, precision=highest) * mean_scale
    products = (basis[:, None, :] * basis[None, :, :]).reshape(36, 3 * node_count)
    damping = (fiber_wide * (1.0 - jnp.tanh(current) ** 2)).reshape(batch_rows, 3 * node_count)
    tangent = (
        fixed_part.reshape(1, 36) - jnp.dot(damping, products.T, precision=highest)
    ) * mean_scale
    return (flat_state, stress, tangent)


def body(
    strain,
    fiber_coeff,
    gradients,
    volume,
    corners,
    rve_worker,
    rve_slot,
    slot_element,
    state_table,
    loading,
    compliance,
):
    elem_rows = strain.shape[0]
    workers = lax.axis_size("rve")
    columns = lax.axis_size("blk")
    capacity = state_table.shape[0]
    slot_cap = (capacity + workers - 1) // workers
    node_count = compliance.shape[1]
    buffer_rows = workers * slot_cap
    network = lax.all_gather(compliance, "rve", axis=0, tiled=True)
    basis = lax.dot_general(
        loading.reshape(18, node_count),
        network,
        (((1,), (1,)), ((), ())),
        preferred_element_type=jnp.float32,
    ).reshape(6, 3 * node_count)
    fixed_part = jnp.dot(
        loading.reshape(6, 3 * node_count).astype(jnp.float32), basis.T, precision=highest
    )
    earlier = (rve_worker[None, :] == rve_worker[:, None]) & (rve_slot[None, :] < rve_slot[:, None])
    home_pos = rve_worker * slot_cap + jnp.sum(earlier, axis=1)
    occupied = slot_element >= 0
    source_home = jnp.where(occupied, slot_element // elem_rows // columns, -1)
    slot_ids = jnp.arange(capacity)
    before = (source_home[None, :] == source_home[:, None]) & (
        slot_ids[None, :] < slot_ids[:, None]
    )
    work_pos = jnp.where(occupied, source_home * slot_cap + jnp.sum(before, axis=1), buffer_rows)
    fetch_pos = jnp.minimum(work_pos, buffer_rows - 1)
    flat_table = state_table.reshape(capacity, 3 * node_count)
    send_strain = jnp.zeros((buffer_rows, 6), jnp.bfloat16).at[home_pos].set(strain)
    send_coeff = jnp.zeros((buffer_rows, node_count), jnp.bfloat16).at[home_pos].set(fiber_coeff)
    got_strain, got_coeff = (
        lax.all_to_all(
            send_strain.reshape(workers, slot_cap, 6),
            "rve",
            split_axis=0,
            concat_axis=0,
            tiled=True,
        ),
        lax.all_to_all(
            send_coeff.reshape(workers, slot_cap, node_count),
            "rve",
            split_axis=0,
            concat_axis=0,
            tiled=True,
        ),
    )
    slot_strain = jnp.where(occupied[:, None], got_strain.reshape(buffer_rows, 6)[fetch_pos], 0)
    slot_coeff = jnp.where(
        occupied[:, None], got_coeff.reshape(buffer_rows, node_count)[fetch_pos], 0
    )
    finals, slot_stress, slot_tangent = micro_solve(
        slot_strain, slot_coeff, flat_table, loading, network, basis, fixed_part
    )
    new_table = jnp.where(occupied[:, None], finals, flat_table)
    back_stress = (
        jnp.zeros((buffer_rows, 6), jnp.float32).at[work_pos].set(slot_stress, mode="drop")
    )
    back_tangent = (
        jnp.zeros((buffer_rows, 36), jnp.float32).at[work_pos].set(slot_tangent, mode="drop")
    )
    ret_stress, ret_tangent = (
        lax.all_to_all(
            back_stress.reshape(workers, slot_cap, 6),
            "rve",
            split_axis=0,
            concat_axis=0,
            tiled=True,
        ),
        lax.all_to_all(
            back_tangent.reshape(workers, slot_cap, 36),
            "rve",
            split_axis=0,
            concat_axis=0,
            tiled=True,
        ),
    )
    stress = ret_stress.reshape(buffer_rows, 6)[home_pos]
    tangent = ret_tangent.reshape(buffer_rows, 36)[home_pos]
    gradient_rows = gradients.reshape(4, 3, elem_rows)
    bmatrix = jnp.einsum("vac,ich->ivah", strain_map(), gradient_rows, precision=highest)
    corner_force = volume * jnp.einsum("ivah,hv->iah", bmatrix, stress, precision=highest)
    corner_block = volume * jnp.einsum(
        "ivah,hvw,iwbh->iabh", bmatrix, tangent.reshape(elem_rows, 6, 6), bmatrix, precision=highest
    )
    contrib = jnp.concatenate([corner_force, corner_block.reshape(4, 9, elem_rows)], axis=1)
    contrib = jnp.transpose(contrib, (1, 0, 2)).reshape(12, 4 * elem_rows)
    device_rank = lax.axis_index("rve") * columns + lax.axis_index("blk")
    local_node = (corners - device_rank * NODE_DEV).reshape(4 * elem_rows)
    onehot = (local_node[:, None] == jnp.arange(2 * NODE_DEV)[None, :]).astype(jnp.float32)
    assembled = jnp.dot(contrib, onehot, precision=highest)
    own_rows = assembled[:, :NODE_DEV] + from_behind(assembled[:, NODE_DEV:], ("rve", "blk"), 1)
    return (new_table.reshape(capacity, 3, node_count), own_rows[:3], own_rows[3:])


ROW = 16
SLOT_PAD = 88
LOAD_PAD = 24


def to_column(row):
    count = row.shape[1]
    grid_row = lax.broadcasted_iota(jnp.int32, (count, count), 0)
    grid_col = lax.broadcasted_iota(jnp.int32, (count, count), 1)
    return jnp.sum(jnp.where(grid_row == grid_col, row, 0), axis=1, keepdims=True)


def home_positions(worker_row, slot_row):
    same = to_column(worker_row) == worker_row
    ahead = to_column(slot_row) < slot_row
    rank = jnp.sum(jnp.where(same & ahead, 1, 0), axis=0, keepdims=True)
    return worker_row * ROW + rank


def home_onehot(worker_row, slot_row, rows):
    positions = home_positions(worker_row, slot_row)
    row_ids = lax.broadcasted_iota(jnp.int32, (rows, positions.shape[1]), 0)
    return (row_ids == positions).astype(jnp.float32)


def work_onehot(source_row, rows):
    count = source_row.shape[1]
    slot_ids = lax.broadcasted_iota(jnp.int32, (count, count), 0)
    later_ids = lax.broadcasted_iota(jnp.int32, (count, count), 1)
    same = to_column(source_row) == source_row
    rank = jnp.sum(jnp.where(same & (slot_ids < later_ids), 1, 0), axis=0, keepdims=True)
    positions = jnp.where(source_row >= 0, source_row * ROW + rank, -1)
    column = to_column(positions)
    lanes = lax.broadcasted_iota(jnp.int32, (count, rows), 1)
    return (lanes == column).astype(jnp.float32)


def dot_nt(left, right, **kwargs):
    return lax.dot_general(
        left, right, (((1,), (1,)), ((), ())), preferred_element_type=jnp.float32, **kwargs
    )


def dot_tn(left, right, **kwargs):
    return lax.dot_general(
        left, right, (((0,), (0,)), ((), ())), preferred_element_type=jnp.float32, **kwargs
    )


def split_wide(values):
    high = values.astype(jnp.bfloat16)
    return high, (values - high.astype(jnp.float32)).astype(jnp.bfloat16)


MESH = pl.DeviceIdType.MESH


def greet(targets):
    barrier = pltpu.get_barrier_semaphore()
    for device in targets:
        pl.semaphore_signal(barrier, inc=1, device_id=device, device_id_type=MESH)
    pl.semaphore_wait(barrier, len(targets))


def exchange(send_ref, recv_ref, send_sems, recv_sems, me, workers):
    copies = []
    for offset in range(1, workers):
        peer = lax.rem(me + offset, workers)
        source = lax.rem(me + workers - offset, workers)
        sent = pltpu.make_async_remote_copy(
            src_ref=send_ref.at[pl.ds(pl.multiple_of(peer * ROW, ROW), ROW)],
            dst_ref=recv_ref.at[pl.ds(pl.multiple_of(me * ROW, ROW), ROW)],
            send_sem=send_sems.at[peer],
            recv_sem=recv_sems.at[me],
            device_id={"rve": peer},
            device_id_type=MESH,
        )
        sent.start()
        landing = recv_ref.at[pl.ds(pl.multiple_of(source * ROW, ROW), ROW)]
        arrival = pltpu.make_async_remote_copy(
            src_ref=landing,
            dst_ref=landing,
            send_sem=send_sems.at[peer],
            recv_sem=recv_sems.at[source],
            device_id={"rve": peer},
            device_id_type=MESH,
        )
        copies.append((sent, arrival))
    here = pl.ds(pl.multiple_of(me * ROW, ROW), ROW)
    recv_ref[here, :] = send_ref[here, :]
    return copies


def gather_kernel(
    strain_ref, fiber_ref, worker_ref, slot_ref, compliance_ref, got_ref, net_ref,
    send_buf, net_send, net_recv, coeff_send, coeff_recv
):
    workers, block, width = net_ref.shape
    near = workers // 2
    quarter = block // 4
    me = lax.axis_index("rve")
    lane = lax.axis_index("blk")
    z, y = me // 2, lax.rem(me, 2)
    x, core = lane // 2, lax.rem(lane, 2)
    routes = (
        {"rve": me + 2},
        {"rve": me - 2},
        {"rve": me + 1 - 2 * y},
        {"blk": lane + 2 - 4 * x},
        {"blk": lane + 1 - 2 * core},
    )
    up, down, across, over, twin = range(5)
    greet(
        [{"rve": lax.rem(me + offset, workers)} for offset in range(1, workers)]
        + [routes[over], routes[twin]]
    )
    for step in range(near):
        column = pl.multiple_of(lax.rem(me + step, workers) * block, block)
        net_ref[me, :, step * block:(step + 1) * block] = compliance_ref[:, pl.ds(column, block)]
    far = pl.multiple_of(lax.rem(me + near, workers) * block, block)
    left = compliance_ref[:, pl.ds(far, block // 2)]
    lower = compliance_ref[block // 2:, pl.ds(far, block)].T
    net_ref[me, :, near * block:] = jnp.where(me < near, left, lower)

    def copy(owner, q, route):
        piece = net_ref.at[owner, pl.ds(pl.multiple_of(q * quarter, quarter), quarter)]
        return pltpu.make_async_remote_copy(
            src_ref=piece,
            dst_ref=piece,
            send_sem=net_send.at[owner, q, route],
            recv_sem=net_recv.at[owner, q],
            device_id=routes[route],
            device_id_type=MESH,
        )

    sends = []

    def push(cond, owner, q, route):
        sends.append((cond, owner, q, route))
        if cond is True:
            copy(owner, q, route).start()
        else:
            pl.when(cond)(lambda: copy(owner, q, route).start())

    def arrive(cond, owner, q):
        if cond is True:
            copy(owner, q, twin).wait_recv()
        else:
            pl.when(cond)(lambda: copy(owner, q, twin).wait_recv())

    k, k2 = 2 * core + x, 2 * core + 1 - x
    has_up, has_down = z < near - 1, z > 0
    push(has_up, me, k, up)
    push(has_down, me, k, down)
    push(True, me, k, across)
    push(has_up, me, k2, up)
    push(has_down, me, k2, down)
    rows = send_buf.shape[0]
    nodes = fiber_ref.shape[1]
    onehot = home_onehot(worker_ref[...], slot_ref[...], rows).astype(jnp.bfloat16)
    send_buf[:, :nodes] = jnp.dot(
        onehot, fiber_ref[...], preferred_element_type=jnp.float32
    ).astype(jnp.bfloat16)
    send_buf[:, nodes:] = dot_nt(onehot, strain_ref[...]).astype(jnp.bfloat16)
    copies = exchange(send_buf, got_ref, coeff_send, coeff_recv, me, workers)

    def lines(distance):
        if distance == 0:
            return [(True, me, None, None)]
        return [
            (z >= distance, me - 2 * distance, up, has_up),
            (z < near - distance, me + 2 * distance, down, has_down),
        ]

    def from_across(distance):
        for has, owner, route, edge in lines(distance):
            other = owner + 1 - 2 * y
            arrive(has, other, k)
            push(has, other, k, over)
            push(has, other, k, twin)

    def from_over(distance):
        for has, owner, route, edge in lines(distance):
            other = owner + 1 - 2 * y
            arrive(has, other, k2)
            push(has, other, k2, twin)

    from_across(0)
    last = near - 1
    for distance in range(1, near):
        for has, owner, route, edge in lines(distance):
            arrive(has, owner, k)
            if distance < last:
                push(has & edge, owner, k, route)
            push(has, owner, k, across)
            if distance == last:
                push(has, owner, k, over)
            push(has, owner, k, twin)
        if distance < last:
            for has, owner, route, edge in lines(distance):
                arrive(has, owner, k2)
                if distance + 1 < last:
                    push(has & edge, owner, k2, route)
                push(has, owner, k2, twin)
        from_over(distance - 1)
        from_across(distance)
    for has, owner, route, edge in lines(last):
        arrive(has, owner, k2)
        push(has, owner, k2, twin)
    from_over(last)
    for offset in range(1, workers):
        owner = lax.rem(me + offset, workers)
        arrive(True, owner, 2 - 2 * core)
        arrive(True, owner, 3 - 2 * core)
    for sent, arrival in copies:
        arrival.wait_recv()
        sent.wait_send()
    for cond, owner, q, route in sends:
        if cond is True:
            copy(owner, q, route).wait_send()
        else:
            pl.when(cond)(lambda: copy(owner, q, route).wait_send())


def micro_kernel(
    got_ref, source_ref, state_ref, loading_ref, halves_ref, new_ref, back_ref,
    dense, forcing, coeff, current, pressure_a, pressure_b
):
    workers, block = halves_ref.shape[0], halves_ref.shape[1]
    nodes = state_ref.shape[2]
    capacity = state_ref.shape[1]
    rows = got_ref.shape[0]
    mean_scale = 1.0 / (3 * nodes)
    near = workers // 2
    for owner in range(workers):
        for step in range(near + 1):
            row, column, width = owner * block, (owner + step) % workers * block, block
            if step == near:
                width = block // 2
                if owner >= near:
                    row, column = column, row + width
            tile = halves_ref[owner, :, step * block:step * block + width]
            dense[row:row + block, column:column + width] = tile
            if step:
                dense[column:column + width, row:row + block] = tile.T
    onehot = work_onehot(source_ref[...], rows)
    onehot = jnp.concatenate(
        [onehot, jnp.zeros((SLOT_PAD - capacity, rows), jnp.float32)], axis=0
    )
    fetch = onehot.astype(jnp.bfloat16)
    slots = jnp.dot(fetch, got_ref[...], preferred_element_type=jnp.float32)
    coeff[...] = slots[:, :nodes]
    strain_rows = slots[:, nodes:nodes + 8].astype(jnp.bfloat16)
    forcing[0:LOAD_PAD, :] = loading_ref[...].astype(jnp.float32)
    current[0:LOAD_PAD, :] = jnp.zeros((LOAD_PAD, nodes), jnp.float32)
    for axis in range(3):
        start = LOAD_PAD + axis * SLOT_PAD
        load = forcing[axis * 8:axis * 8 + 8, :].astype(jnp.bfloat16)
        forcing[start:start + SLOT_PAD, :] = jnp.dot(
            strain_rows, load, preferred_element_type=jnp.float32
        )
        current[start + 80:start + SLOT_PAD, :] = jnp.zeros((SLOT_PAD - 80, nodes), jnp.float32)
        current[start:start + capacity, :] = state_ref[axis]

    def press(values, lanes):
        c = coeff[:, lanes]
        wide = jnp.concatenate([jnp.zeros((LOAD_PAD, c.shape[1]), jnp.float32), c, c, c], axis=0)
        return (forcing[:, lanes] - wide * jnp.tanh(values)).astype(jnp.bfloat16)

    for tile in range(nodes // block):
        lanes = slice(tile * block, (tile + 1) * block)
        pressure_a[:, lanes] = press(current[:, lanes], lanes)
    for iteration in range(ITERS):
        reads, writes = (pressure_a, pressure_b) if iteration % 2 == 0 else (pressure_b, pressure_a)
        for tile in range(nodes // block):
            lanes = slice(tile * block, (tile + 1) * block)
            values = jnp.dot(reads[...], dense[:, lanes], preferred_element_type=jnp.float32)
            if iteration == ITERS - 1:
                current[:, lanes] = values
            else:
                writes[:, lanes] = press(values, lanes)

    occupied = jnp.sum(onehot, axis=1, keepdims=True) > 0.5
    tangent = jnp.zeros((SLOT_PAD, 96), jnp.float32)
    tangent_low = jnp.zeros((SLOT_PAD, 48), jnp.float32)
    stress = jnp.zeros((SLOT_PAD, 8), jnp.float32)
    fixed = jnp.zeros((8, 8), jnp.float32)
    for axis in range(3):
        start = LOAD_PAD + axis * SLOT_PAD
        final = current[start:start + SLOT_PAD, :]
        new_ref[axis] = jnp.where(
            occupied[:capacity], current[start:start + capacity, :], state_ref[axis]
        )
        basis = current[axis * 8:axis * 8 + 8, :]
        load = forcing[axis * 8:axis * 8 + 8, :].astype(jnp.bfloat16)
        products = jnp.concatenate([basis[k:k + 1, :] * basis for k in range(6)], axis=0)
        products_high, products_low = split_wide(products)
        damping = coeff[...] * (1.0 - jnp.tanh(final) ** 2)
        damping_high, damping_low = split_wide(damping)
        tangent += dot_nt(damping_high, jnp.concatenate([products_high, products_low], axis=0))
        tangent_low += dot_nt(damping_low, products_high)
        final_high, final_low = split_wide(final)
        stress += dot_nt(final_high, load) + dot_nt(final_low, load)
        basis_high, basis_low = split_wide(basis)
        fixed += dot_nt(load, basis_high) + dot_nt(load, basis_low)
    lane_ids = lax.broadcasted_iota(jnp.int32, (8, 48), 1)
    row_ids = lax.broadcasted_iota(jnp.int32, (8, 48), 0)
    spread = jnp.dot(
        fixed, (lane_ids % 8 == row_ids).astype(jnp.float32), precision=highest,
        preferred_element_type=jnp.float32,
    )
    fixed_row = jnp.sum(jnp.where(lane_ids // 8 == row_ids, spread, 0.0), axis=0, keepdims=True)
    total = fixed_row - (tangent[:, :48] + tangent[:, 48:] + tangent_low)
    packed = jnp.concatenate(
        [total, stress, jnp.zeros((SLOT_PAD, 72), jnp.float32)], axis=1
    ) * mean_scale
    back_ref[...] = dot_tn(onehot, packed, precision=highest)


def assemble_kernel(
    back_ref, worker_ref, slot_ref, gradient_ref, volume_ref, corner_ref, own_ref,
    ret_ref, next_buf, prev_buf, ret_send, ret_recv, shift_sems
):
    rows = ret_ref.shape[0]
    workers, columns = lax.axis_size("rve"), lax.axis_size("blk")
    me, lane = lax.axis_index("rve"), lax.axis_index("blk")
    rank = me * columns + lane
    ahead, behind = lax.rem(rank + 1, workers * columns), lax.rem(
        rank + workers * columns - 1, workers * columns
    )
    following = {"rve": ahead // columns, "blk": lax.rem(ahead, columns)}
    leading = {"rve": behind // columns, "blk": lax.rem(behind, columns)}
    greet(
        [{"rve": lax.rem(me + offset, workers)} for offset in range(1, workers)]
        + [following, leading]
    )
    copies = exchange(back_ref, ret_ref, ret_send, ret_recv, me, workers)
    for sent, arrival in copies:
        arrival.wait_recv()
    onehot = home_onehot(worker_ref[...], slot_ref[...], rows)
    values = dot_tn(ret_ref[...], onehot, precision=highest)
    volume = volume_ref[...]
    count = volume.shape[1]
    stress = [values[48 + k:49 + k, :] for k in range(6)]
    rows_of = [values[k * 8:k * 8 + 8, :] for k in range(6)]
    node_ids = lax.broadcasted_iota(jnp.int32, (2 * NODE_DEV, count), 0)
    assembled = jnp.zeros((16, 2 * NODE_DEV), jnp.float32)

    def apply(g, terms):
        gx, gy, gz = g
        return (
            gx * terms[0] + gz * terms[4] + gy * terms[5],
            gy * terms[1] + gz * terms[3] + gx * terms[5],
            gz * terms[2] + gy * terms[3] + gx * terms[4],
        )

    for corner in range(4):
        g = [gradient_ref[3 * corner + c:3 * corner + c + 1, :] for c in range(3)]
        lines = [volume * f for f in apply(g, stress)]
        for u in apply(g, rows_of):
            lines += [volume * m for m in apply(g, [u[j:j + 1, :] for j in range(6)])]
        contrib = jnp.concatenate(lines + [jnp.zeros((4, count), jnp.float32)], axis=0)
        picked = (node_ids == corner_ref[corner:corner + 1, :] - rank * NODE_DEV).astype(jnp.float32)
        assembled += dot_nt(contrib, picked, precision=highest)
    next_buf[...] = assembled[:, NODE_DEV:]
    shift = pltpu.make_async_remote_copy(
        src_ref=next_buf, dst_ref=prev_buf, send_sem=shift_sems.at[0], recv_sem=shift_sems.at[1],
        device_id=following, device_id_type=MESH,
    )
    shift.start()
    for sent, arrival in copies:
        sent.wait_send()
    shift.wait()
    own_ref[...] = assembled[:, :NODE_DEV] + jnp.where(rank > 0, prev_buf[...], 0.0)


def tiled_body(
    strain, fiber_coeff, gradients, volume, corners, rve_worker, rve_slot, slot_element,
    state_table, loading, compliance,
):
    elem_rows = strain.shape[0]
    workers = lax.axis_size("rve")
    columns = lax.axis_size("blk")
    capacity = state_table.shape[0]
    nodes = compliance.shape[1]
    block = compliance.shape[0]
    rows = workers * ROW
    vmem = pl.BlockSpec(memory_space=pltpu.VMEM)
    params = pltpu.CompilerParams(vmem_limit_bytes=56 * 2**20)
    worker_row, slot_row = rve_worker[None, :], rve_slot[None, :]
    strain_lanes = jnp.pad(strain.T, ((0, 122), (0, 0)))
    got, halves = pl.pallas_call(
        gather_kernel,
        out_shape=(
            jax.ShapeDtypeStruct((rows, nodes + 128), jnp.bfloat16),
            jax.ShapeDtypeStruct((workers, block, workers // 2 * block + block // 2), jnp.bfloat16),
        ),
        in_specs=[vmem] * 5, out_specs=(vmem, vmem),
        scratch_shapes=[
            pltpu.VMEM((rows, nodes + 128), jnp.bfloat16),
            pltpu.SemaphoreType.DMA((workers, 4, 5)),
            pltpu.SemaphoreType.DMA((workers, 4)),
            pltpu.SemaphoreType.DMA((workers,)),
            pltpu.SemaphoreType.DMA((workers,)),
        ],
        compiler_params=pltpu.CompilerParams(
            vmem_limit_bytes=40 * 2**20, collective_id=0, has_side_effects=True
        ),
        name="gather",
    )(strain_lanes, fiber_coeff, worker_row, slot_row, compliance)
    source = jnp.where(slot_element >= 0, slot_element // (elem_rows * columns), -1)[None, :]
    load_rows = jnp.pad(jnp.transpose(loading, (1, 0, 2)), ((0, 0), (0, 2), (0, 0)))
    load_rows = load_rows.reshape(LOAD_PAD, nodes)
    total_rows = LOAD_PAD + 3 * SLOT_PAD
    new_table, back = pl.pallas_call(
        micro_kernel,
        out_shape=(
            jax.ShapeDtypeStruct((3, capacity, nodes), jnp.float32),
            jax.ShapeDtypeStruct((rows, 128), jnp.float32),
        ),
        in_specs=[vmem] * 5, out_specs=(vmem, vmem),
        scratch_shapes=[
            pltpu.VMEM((nodes, nodes), jnp.bfloat16),
            pltpu.VMEM((total_rows, nodes), jnp.float32),
            pltpu.VMEM((SLOT_PAD, nodes), jnp.float32),
            pltpu.VMEM((total_rows, nodes), jnp.float32),
            pltpu.VMEM((total_rows, nodes), jnp.bfloat16),
            pltpu.VMEM((total_rows, nodes), jnp.bfloat16),
        ],
        compiler_params=params, name="micro",
    )(got, source, jnp.transpose(state_table, (1, 0, 2)), load_rows, halves)
    own_rows = pl.pallas_call(
        assemble_kernel,
        out_shape=jax.ShapeDtypeStruct((16, NODE_DEV), jnp.float32),
        in_specs=[vmem] * 6, out_specs=vmem,
        scratch_shapes=[
            pltpu.VMEM((rows, 128), jnp.float32),
            pltpu.VMEM((16, NODE_DEV), jnp.float32),
            pltpu.VMEM((16, NODE_DEV), jnp.float32),
            pltpu.SemaphoreType.DMA((workers,)),
            pltpu.SemaphoreType.DMA((workers,)),
            pltpu.SemaphoreType.DMA((2,)),
        ],
        compiler_params=pltpu.CompilerParams(
            vmem_limit_bytes=16 * 2**20, collective_id=1, has_side_effects=True
        ),
        name="assemble",
    )(back, worker_row, slot_row, gradients, volume[None, :], corners)
    return jnp.transpose(new_table, (1, 0, 2)), own_rows[:3], own_rows[3:12]


def solution(mesh):
    def chosen(*args):
        workers, columns = lax.axis_size("rve"), lax.axis_size("blk")
        block = args[-1].shape[0]
        even = workers == 8 and columns == 4 and block % 256 == 0
        few = -(-args[8].shape[0] // workers) <= ROW and args[8].shape[0] <= SLOT_PAD
        return (tiled_body if even and few else body)(*args)

    return jax.shard_map(
        chosen,
        mesh=mesh,
        in_specs=(
            P(("rve", "blk"), None),
            P(("rve", "blk"), None),
            P(None, ("rve", "blk")),
            P(("rve", "blk")),
            P(None, ("rve", "blk")),
            P(("rve", "blk")),
            P(("rve", "blk")),
            P(("rve", "blk")),
            P(("rve", "blk"), None, None),
            P(),
            P("rve", None),
        ),
        out_specs=(P(("rve", "blk"), None, None), P(None, ("rve", "blk")), P(None, ("rve", "blk"))),
        check_vma=False,
    )
```

```python
import jax
import jax.numpy as jnp
import numpy as np
from jax import lax
from jax.experimental import pallas as pl
from jax.experimental.pallas import tpu as pltpu
from jax.sharding import PartitionSpec as P

ITERS = 3
NODE_DEV = 128


highest = lax.Precision.HIGHEST


def from_behind(block, axis, distance):
    devices = range(lax.axis_size(axis))
    route = [(i - distance, i) for i in devices if i - distance in devices]
    return lax.ppermute(block, axis, route)


def strain_map():
    voigt_map = np.zeros((6, 3, 3), np.float32)
    for voigt_row, first_axis, second_axis in (
        (0, 0, 0),
        (1, 1, 1),
        (2, 2, 2),
        (3, 1, 2),
        (3, 2, 1),
        (4, 0, 2),
        (4, 2, 0),
        (5, 0, 1),
        (5, 1, 0),
    ):
        voigt_map[voigt_row, first_axis, second_axis] = 1.0
    return jnp.asarray(voigt_map)


def micro_solve(strain_rows, coeff_rows, start_rows, loading, network, basis, fixed_part):
    batch_rows = strain_rows.shape[0]
    node_count = network.shape[0]
    mean_scale = 1.0 / (3 * node_count)
    forcing = jnp.dot(
        strain_rows, loading.reshape(6, 3 * node_count), preferred_element_type=jnp.float32
    ).reshape(batch_rows, 3, node_count)
    fiber_wide = coeff_rows[:, None, :].astype(jnp.float32)
    current = start_rows.reshape(batch_rows, 3, node_count)
    for iteration in range(ITERS):
        pressure = (
            (forcing - fiber_wide * jnp.tanh(current))
            .astype(jnp.bfloat16)
            .reshape(batch_rows * 3, node_count)
        )
        current = lax.dot_general(
            pressure, network, (((1,), (1,)), ((), ())), preferred_element_type=jnp.float32
        ).reshape(batch_rows, 3, node_count)
    flat_state = current.reshape(batch_rows, 3 * node_count)
    load_float = loading.reshape(6, 3 * node_count).astype(jnp.float32)
    stress = jnp.dot(flat_state, load_float.T, precision=highest) * mean_scale
    products = (basis[:, None, :] * basis[None, :, :]).reshape(36, 3 * node_count)
    damping = (fiber_wide * (1.0 - jnp.tanh(current) ** 2)).reshape(batch_rows, 3 * node_count)
    tangent = (
        fixed_part.reshape(1, 36) - jnp.dot(damping, products.T, precision=highest)
    ) * mean_scale
    return (flat_state, stress, tangent)


def body(
    strain,
    fiber_coeff,
    gradients,
    volume,
    corners,
    rve_worker,
    rve_slot,
    slot_element,
    state_table,
    loading,
    compliance,
):
    elem_rows = strain.shape[0]
    workers = lax.axis_size("rve")
    columns = lax.axis_size("blk")
    capacity = state_table.shape[0]
    slot_cap = (capacity + workers - 1) // workers
    node_count = compliance.shape[1]
    buffer_rows = workers * slot_cap
    network = lax.all_gather(compliance, "rve", axis=0, tiled=True)
    basis = lax.dot_general(
        loading.reshape(18, node_count),
        network,
        (((1,), (1,)), ((), ())),
        preferred_element_type=jnp.float32,
    ).reshape(6, 3 * node_count)
    fixed_part = jnp.dot(
        loading.reshape(6, 3 * node_count).astype(jnp.float32), basis.T, precision=highest
    )
    earlier = (rve_worker[None, :] == rve_worker[:, None]) & (rve_slot[None, :] < rve_slot[:, None])
    home_pos = rve_worker * slot_cap + jnp.sum(earlier, axis=1)
    occupied = slot_element >= 0
    source_home = jnp.where(occupied, slot_element // elem_rows // columns, -1)
    slot_ids = jnp.arange(capacity)
    before = (source_home[None, :] == source_home[:, None]) & (
        slot_ids[None, :] < slot_ids[:, None]
    )
    work_pos = jnp.where(occupied, source_home * slot_cap + jnp.sum(before, axis=1), buffer_rows)
    fetch_pos = jnp.minimum(work_pos, buffer_rows - 1)
    flat_table = state_table.reshape(capacity, 3 * node_count)
    send_strain = jnp.zeros((buffer_rows, 6), jnp.bfloat16).at[home_pos].set(strain)
    send_coeff = jnp.zeros((buffer_rows, node_count), jnp.bfloat16).at[home_pos].set(fiber_coeff)
    got_strain, got_coeff = (
        lax.all_to_all(
            send_strain.reshape(workers, slot_cap, 6),
            "rve",
            split_axis=0,
            concat_axis=0,
            tiled=True,
        ),
        lax.all_to_all(
            send_coeff.reshape(workers, slot_cap, node_count),
            "rve",
            split_axis=0,
            concat_axis=0,
            tiled=True,
        ),
    )
    slot_strain = jnp.where(occupied[:, None], got_strain.reshape(buffer_rows, 6)[fetch_pos], 0)
    slot_coeff = jnp.where(
        occupied[:, None], got_coeff.reshape(buffer_rows, node_count)[fetch_pos], 0
    )
    finals, slot_stress, slot_tangent = micro_solve(
        slot_strain, slot_coeff, flat_table, loading, network, basis, fixed_part
    )
    new_table = jnp.where(occupied[:, None], finals, flat_table)
    back_stress = (
        jnp.zeros((buffer_rows, 6), jnp.float32).at[work_pos].set(slot_stress, mode="drop")
    )
    back_tangent = (
        jnp.zeros((buffer_rows, 36), jnp.float32).at[work_pos].set(slot_tangent, mode="drop")
    )
    ret_stress, ret_tangent = (
        lax.all_to_all(
            back_stress.reshape(workers, slot_cap, 6),
            "rve",
            split_axis=0,
            concat_axis=0,
            tiled=True,
        ),
        lax.all_to_all(
            back_tangent.reshape(workers, slot_cap, 36),
            "rve",
            split_axis=0,
            concat_axis=0,
            tiled=True,
        ),
    )
    stress = ret_stress.reshape(buffer_rows, 6)[home_pos]
    tangent = ret_tangent.reshape(buffer_rows, 36)[home_pos]
    gradient_rows = gradients.reshape(4, 3, elem_rows)
    bmatrix = jnp.einsum("vac,ich->ivah", strain_map(), gradient_rows, precision=highest)
    corner_force = volume * jnp.einsum("ivah,hv->iah", bmatrix, stress, precision=highest)
    corner_block = volume * jnp.einsum(
        "ivah,hvw,iwbh->iabh", bmatrix, tangent.reshape(elem_rows, 6, 6), bmatrix, precision=highest
    )
    contrib = jnp.concatenate([corner_force, corner_block.reshape(4, 9, elem_rows)], axis=1)
    contrib = jnp.transpose(contrib, (1, 0, 2)).reshape(12, 4 * elem_rows)
    device_rank = lax.axis_index("rve") * columns + lax.axis_index("blk")
    local_node = (corners - device_rank * NODE_DEV).reshape(4 * elem_rows)
    onehot = (local_node[:, None] == jnp.arange(2 * NODE_DEV)[None, :]).astype(jnp.float32)
    assembled = jnp.dot(contrib, onehot, precision=highest)
    own_rows = assembled[:, :NODE_DEV] + from_behind(assembled[:, NODE_DEV:], ("rve", "blk"), 1)
    return (new_table.reshape(capacity, 3, node_count), own_rows[:3], own_rows[3:])


ROW = 16
SLOT_PAD = 88
LOAD_PAD = 24


def to_column(row):
    count = row.shape[1]
    grid_row = lax.broadcasted_iota(jnp.int32, (count, count), 0)
    grid_col = lax.broadcasted_iota(jnp.int32, (count, count), 1)
    return jnp.sum(jnp.where(grid_row == grid_col, row, 0), axis=1, keepdims=True)


def home_positions(worker_row, slot_row):
    same = to_column(worker_row) == worker_row
    ahead = to_column(slot_row) < slot_row
    rank = jnp.sum(jnp.where(same & ahead, 1, 0), axis=0, keepdims=True)
    return worker_row * ROW + rank


def home_onehot(worker_row, slot_row, rows):
    positions = home_positions(worker_row, slot_row)
    row_ids = lax.broadcasted_iota(jnp.int32, (rows, positions.shape[1]), 0)
    return (row_ids == positions).astype(jnp.float32)


def work_onehot(source_row, rows):
    count = source_row.shape[1]
    slot_ids = lax.broadcasted_iota(jnp.int32, (count, count), 0)
    later_ids = lax.broadcasted_iota(jnp.int32, (count, count), 1)
    same = to_column(source_row) == source_row
    rank = jnp.sum(jnp.where(same & (slot_ids < later_ids), 1, 0), axis=0, keepdims=True)
    positions = jnp.where(source_row >= 0, source_row * ROW + rank, -1)
    column = to_column(positions)
    lanes = lax.broadcasted_iota(jnp.int32, (count, rows), 1)
    return (lanes == column).astype(jnp.float32)


def dot_nt(left, right, **kwargs):
    return lax.dot_general(
        left, right, (((1,), (1,)), ((), ())), preferred_element_type=jnp.float32, **kwargs
    )


def dot_tn(left, right, **kwargs):
    return lax.dot_general(
        left, right, (((0,), (0,)), ((), ())), preferred_element_type=jnp.float32, **kwargs
    )


def split_wide(values):
    high = values.astype(jnp.bfloat16)
    return high, (values - high.astype(jnp.float32)).astype(jnp.bfloat16)


MESH = pl.DeviceIdType.MESH


def greet(targets):
    barrier = pltpu.get_barrier_semaphore()
    for device in targets:
        pl.semaphore_signal(barrier, inc=1, device_id=device, device_id_type=MESH)
    pl.semaphore_wait(barrier, len(targets))


def exchange(send_ref, recv_ref, send_sems, recv_sems, me, workers):
    copies = []
    for offset in range(1, workers):
        peer = lax.rem(me + offset, workers)
        source = lax.rem(me + workers - offset, workers)
        sent = pltpu.make_async_remote_copy(
            src_ref=send_ref.at[pl.ds(pl.multiple_of(peer * ROW, ROW), ROW)],
            dst_ref=recv_ref.at[pl.ds(pl.multiple_of(me * ROW, ROW), ROW)],
            send_sem=send_sems.at[peer],
            recv_sem=recv_sems.at[me],
            device_id={"rve": peer},
            device_id_type=MESH,
        )
        sent.start()
        landing = recv_ref.at[pl.ds(pl.multiple_of(source * ROW, ROW), ROW)]
        arrival = pltpu.make_async_remote_copy(
            src_ref=landing,
            dst_ref=landing,
            send_sem=send_sems.at[peer],
            recv_sem=recv_sems.at[source],
            device_id={"rve": peer},
            device_id_type=MESH,
        )
        copies.append((sent, arrival))
    here = pl.ds(pl.multiple_of(me * ROW, ROW), ROW)
    recv_ref[here, :] = send_ref[here, :]
    return copies


def step_kernel(
    strain_hbm, fiber_hbm, gradient_hbm, volume_hbm, corner_hbm, worker_hbm, slot_hbm, element_hbm,
    state_hbm, loading_hbm, compliance_hbm, new_hbm, force_ref, block_ref,
    strain_ref, fiber_ref, gradient_ref, volume_ref, corner_ref, worker_ref, slot_ref, element_ref,
    state_ref, loading_ref, left_ref, lower_ref, got_ref, net_ref, send_buf,
    dense, forcing, coeff, current, pressure_a, pressure_b, back_ref, ret_ref, next_buf, prev_buf,
    load_sems, net_send, net_recv, coeff_send, coeff_recv, ret_send, ret_recv, shift_sems
):
    workers, block, width = net_ref.shape
    columns = lax.axis_size("blk")
    near = workers // 2
    quarter = block // 4
    nodes = compliance_hbm.shape[1]
    elem_rows = fiber_hbm.shape[0]
    capacity = state_hbm.shape[1]
    rows = send_buf.shape[0]
    mean_scale = 1.0 / (3 * nodes)
    me = lax.axis_index("rve")
    lane = lax.axis_index("blk")
    z, y = me // 2, lax.rem(me, 2)
    x, core = lane // 2, lax.rem(lane, 2)
    rank = me * columns + lane
    ahead = lax.rem(rank + 1, workers * columns)
    behind = lax.rem(rank + workers * columns - 1, workers * columns)
    following = {"rve": ahead // columns, "blk": lax.rem(ahead, columns)}
    leading = {"rve": behind // columns, "blk": lax.rem(behind, columns)}
    routes = (
        {"rve": me + 2},
        {"rve": me - 2},
        {"rve": me + 1 - 2 * y},
        {"blk": lane + 2 - 4 * x},
        {"blk": lane + 1 - 2 * core},
    )
    up, down, across, over, twin = range(5)
    far = pl.multiple_of(lax.rem(me + near, workers) * block, block)
    own_slab = []
    for step in range(near):
        column = pl.multiple_of(lax.rem(me + step, workers) * block, block)
        own_slab.append((
            compliance_hbm.at[:, pl.ds(column, block)],
            net_ref.at[me, :, pl.ds(step * block, block)],
        ))
    own_slab += [
        (compliance_hbm.at[:, pl.ds(far, block // 2)], left_ref),
        (compliance_hbm.at[pl.ds(block // 2, block // 2), pl.ds(far, block)], lower_ref),
    ]
    packs = [
        (strain_hbm, strain_ref), (fiber_hbm, fiber_ref), (worker_hbm, worker_ref),
        (slot_hbm, slot_ref),
    ]
    laters = [
        (element_hbm, element_ref), (loading_hbm, loading_ref), (state_hbm, state_ref),
        (gradient_hbm, gradient_ref), (volume_hbm, volume_ref), (corner_hbm, corner_ref),
    ]
    loads = [
        pltpu.make_async_copy(src, dst, load_sems.at[at])
        for at, (src, dst) in enumerate(own_slab + packs + laters)
    ]
    for load in loads:
        load.start()
    slab_loads, pack_loads = loads[:len(own_slab)], loads[len(own_slab):len(own_slab) + len(packs)]
    later_loads = loads[len(own_slab) + len(packs):]
    greet(
        [{"rve": lax.rem(me + offset, workers)} for offset in range(1, workers)]
        + [routes[over], routes[twin], following, leading]
    )
    for load in slab_loads:
        load.wait()
    net_ref[me, :, near * block:] = jnp.where(me < near, left_ref[...], lower_ref[...].T)

    def copy(owner, q, route):
        piece = net_ref.at[owner, pl.ds(pl.multiple_of(q * quarter, quarter), quarter)]
        return pltpu.make_async_remote_copy(
            src_ref=piece,
            dst_ref=piece,
            send_sem=net_send.at[owner, q, route],
            recv_sem=net_recv.at[owner, q],
            device_id=routes[route],
            device_id_type=MESH,
        )

    sends = []

    def push(cond, owner, q, route):
        sends.append((cond, owner, q, route))
        if cond is True:
            copy(owner, q, route).start()
        else:
            pl.when(cond)(lambda: copy(owner, q, route).start())

    def arrive(cond, owner, q):
        if cond is True:
            copy(owner, q, twin).wait_recv()
        else:
            pl.when(cond)(lambda: copy(owner, q, twin).wait_recv())

    k, k2 = 2 * core + x, 2 * core + 1 - x
    has_up, has_down = z < near - 1, z > 0
    push(has_up, me, k, up)
    push(has_down, me, k, down)
    push(True, me, k, across)
    push(has_up, me, k2, up)
    push(has_down, me, k2, down)
    for load in pack_loads:
        load.wait()
    home = home_onehot(worker_ref[...], slot_ref[...], rows)
    home_bf16 = home.astype(jnp.bfloat16)
    send_buf[:, :nodes] = jnp.dot(
        home_bf16, fiber_ref[...], preferred_element_type=jnp.float32
    ).astype(jnp.bfloat16)
    send_buf[:, nodes:] = jnp.zeros((rows, 128), jnp.bfloat16)
    send_buf[:, nodes:nodes + 6] = dot_nt(home_bf16, strain_ref[...]).astype(jnp.bfloat16)
    copies = exchange(send_buf, got_ref, coeff_send, coeff_recv, me, workers)

    def lines(distance):
        if distance == 0:
            return [(True, me, None, None)]
        return [
            (z >= distance, me - 2 * distance, up, has_up),
            (z < near - distance, me + 2 * distance, down, has_down),
        ]

    def from_across(distance):
        for has, owner, route, edge in lines(distance):
            other = owner + 1 - 2 * y
            arrive(has, other, k)
            push(has, other, k, over)
            push(has, other, k, twin)

    def from_over(distance):
        for has, owner, route, edge in lines(distance):
            other = owner + 1 - 2 * y
            arrive(has, other, k2)
            push(has, other, k2, twin)

    def place(owner):
        rows_here = pl.ds(pl.multiple_of(owner * block, block), block)
        for step in range(near):
            there = pl.ds(pl.multiple_of(lax.rem(owner + step, workers) * block, block), block)
            tile = net_ref[owner, :, step * block:(step + 1) * block]
            dense[rows_here, there] = tile
            if step:
                dense[there, rows_here] = tile.T
        tile = net_ref[owner, :, near * block:]
        low = owner < near
        row = pl.multiple_of(jnp.where(low, owner, owner - near) * block, block)
        half = block // 2
        column = pl.multiple_of(jnp.where(low, (owner + near) * block, owner * block + half), half)
        dense[pl.ds(row, block), pl.ds(column, half)] = tile
        dense[pl.ds(column, half), pl.ds(row, block)] = tile.T

    def finish(z_other, y_other):
        owner = z_other * 2 + y_other
        arrive(True, owner, 2 - 2 * core)
        arrive(True, owner, 3 - 2 * core)
        place(owner)

    def setup():
        for load in later_loads:
            load.wait()
        for sent, arrival in copies:
            arrival.wait_recv()
        element_row = element_ref[...]
        source = jnp.full(element_row.shape, -1, jnp.int32)
        for worker in range(workers):
            source += jnp.where(element_row >= worker * elem_rows * columns, 1, 0)
        onehot = work_onehot(source, rows)
        onehot = jnp.concatenate(
            [onehot, jnp.zeros((SLOT_PAD - capacity, rows), jnp.float32)], axis=0
        )
        slots = jnp.dot(
            onehot.astype(jnp.bfloat16), got_ref[...], preferred_element_type=jnp.float32
        )
        coeff[...] = slots[:, :nodes]
        strain_rows = slots[:, nodes:nodes + 8].astype(jnp.bfloat16)
        forcing[0:LOAD_PAD, :] = jnp.zeros((LOAD_PAD, nodes), jnp.float32)
        for k_load in range(6):
            three = loading_ref[k_load].astype(jnp.float32)
            for axis in range(3):
                forcing[axis * 8 + k_load:axis * 8 + k_load + 1, :] = three[axis:axis + 1, :]
        current[0:LOAD_PAD, :] = jnp.zeros((LOAD_PAD, nodes), jnp.float32)
        for axis in range(3):
            start = LOAD_PAD + axis * SLOT_PAD
            load_rows = forcing[axis * 8:axis * 8 + 8, :].astype(jnp.bfloat16)
            forcing[start:start + SLOT_PAD, :] = jnp.dot(
                strain_rows, load_rows, preferred_element_type=jnp.float32
            )
            current[start + 80:start + SLOT_PAD, :] = jnp.zeros((SLOT_PAD - 80, nodes), jnp.float32)
            current[start:start + capacity, :] = state_ref[axis]
        for tile in range(nodes // block):
            lanes = slice(tile * block, (tile + 1) * block)
            pressure_a[:, lanes] = press(current[:, lanes], lanes)
        return onehot

    def press(values, lanes):
        c = coeff[:, lanes]
        wide = jnp.concatenate([jnp.zeros((LOAD_PAD, c.shape[1]), jnp.float32), c, c, c], axis=0)
        return (forcing[:, lanes] - wide * jnp.tanh(values)).astype(jnp.bfloat16)

    last = near - 1
    full = 1
    z_one = z + 1 - 2 * lax.rem(z, 2)
    z_two = lax.rem(z + 2, near)
    z_three = last - z

    def from_over_line(distance):
        for has, owner, route, edge in lines(distance):
            arrive(has, owner, k2)
            push(has, owner, k2, twin)

    from_across(0)
    place(me)
    for distance in range(1, near):
        for has, owner, route, edge in lines(distance):
            arrive(has, owner, k)
            if distance < last:
                push(has & edge, owner, k, route)
            push(has, owner, k, across)
            if distance > full:
                push(has, owner, k, over)
            push(has, owner, k, twin)
        if distance <= full:
            for has, owner, route, edge in lines(distance):
                arrive(has, owner, k2)
                if distance + 1 <= full:
                    push(has & edge, owner, k2, route)
                push(has, owner, k2, twin)
        from_over(distance - 1)
        if distance - 1 > full:
            from_over_line(distance - 1)
        from_across(distance)
        if distance == 2:
            finish(z, 1 - y)
    onehot = setup()
    finish(z_one, y)
    from_over_line(last)
    from_over(last)
    finish(z_one, 1 - y)
    for z_other in (z_two, z_three):
        finish(z_other, y)
        finish(z_other, 1 - y)

    for iteration in range(ITERS):
        reads, writes = (pressure_a, pressure_b) if iteration % 2 == 0 else (pressure_b, pressure_a)
        for tile in range(nodes // block):
            lanes = slice(tile * block, (tile + 1) * block)
            values = jnp.dot(reads[...], dense[:, lanes], preferred_element_type=jnp.float32)
            if iteration == ITERS - 1:
                current[:, lanes] = values
            else:
                writes[:, lanes] = press(values, lanes)

    occupied = jnp.sum(onehot, axis=1, keepdims=True) > 0.5
    tangent = jnp.zeros((SLOT_PAD, 96), jnp.float32)
    tangent_low = jnp.zeros((SLOT_PAD, 48), jnp.float32)
    stress = jnp.zeros((SLOT_PAD, 8), jnp.float32)
    fixed = jnp.zeros((8, 8), jnp.float32)
    for axis in range(3):
        start = LOAD_PAD + axis * SLOT_PAD
        final = current[start:start + SLOT_PAD, :]
        state_ref[axis] = jnp.where(
            occupied[:capacity], current[start:start + capacity, :], state_ref[axis]
        )
        basis = current[axis * 8:axis * 8 + 8, :]
        load = forcing[axis * 8:axis * 8 + 8, :].astype(jnp.bfloat16)
        products = jnp.concatenate([basis[k:k + 1, :] * basis for k in range(6)], axis=0)
        products_high, products_low = split_wide(products)
        damping = coeff[...] * (1.0 - jnp.tanh(final) ** 2)
        damping_high, damping_low = split_wide(damping)
        tangent += dot_nt(damping_high, jnp.concatenate([products_high, products_low], axis=0))
        tangent_low += dot_nt(damping_low, products_high)
        final_high, final_low = split_wide(final)
        stress += dot_nt(final_high, load) + dot_nt(final_low, load)
        basis_high, basis_low = split_wide(basis)
        fixed += dot_nt(load, basis_high) + dot_nt(load, basis_low)
    store = pltpu.make_async_copy(state_ref, new_hbm, load_sems.at[len(loads)])
    store.start()
    lane_ids = lax.broadcasted_iota(jnp.int32, (8, 48), 1)
    row_ids = lax.broadcasted_iota(jnp.int32, (8, 48), 0)
    spread = jnp.dot(
        fixed, (lane_ids % 8 == row_ids).astype(jnp.float32), precision=highest,
        preferred_element_type=jnp.float32,
    )
    fixed_row = jnp.sum(jnp.where(lane_ids // 8 == row_ids, spread, 0.0), axis=0, keepdims=True)
    total = fixed_row - (tangent[:, :48] + tangent[:, 48:] + tangent_low)
    packed = jnp.concatenate(
        [total, stress, jnp.zeros((SLOT_PAD, 72), jnp.float32)], axis=1
    ) * mean_scale
    back_ref[...] = dot_tn(onehot, packed, precision=highest)
    returns = exchange(back_ref, ret_ref, ret_send, ret_recv, me, workers)
    for sent, arrival in copies:
        sent.wait_send()
    for cond, owner, q, route in sends:
        if cond is True:
            copy(owner, q, route).wait_send()
        else:
            pl.when(cond)(lambda: copy(owner, q, route).wait_send())
    for sent, arrival in returns:
        arrival.wait_recv()
    values = dot_tn(ret_ref[...], home, precision=highest)
    volume = volume_ref[...]
    count = volume.shape[1]
    stress = [values[48 + k:49 + k, :] for k in range(6)]
    rows_of = [values[k * 8:k * 8 + 8, :] for k in range(6)]
    node_ids = lax.broadcasted_iota(jnp.int32, (2 * NODE_DEV, count), 0)
    assembled = jnp.zeros((16, 2 * NODE_DEV), jnp.float32)

    def apply(g, terms):
        gx, gy, gz = g
        return (
            gx * terms[0] + gz * terms[4] + gy * terms[5],
            gy * terms[1] + gz * terms[3] + gx * terms[5],
            gz * terms[2] + gy * terms[3] + gx * terms[4],
        )

    for corner in range(4):
        g = [gradient_ref[3 * corner + c:3 * corner + c + 1, :] for c in range(3)]
        lines = [volume * f for f in apply(g, stress)]
        for u in apply(g, rows_of):
            lines += [volume * m for m in apply(g, [u[j:j + 1, :] for j in range(6)])]
        contrib = jnp.concatenate(lines + [jnp.zeros((4, count), jnp.float32)], axis=0)
        picked = (node_ids == corner_ref[corner:corner + 1, :] - rank * NODE_DEV).astype(jnp.float32)
        assembled += dot_nt(contrib, picked, precision=highest)
    next_buf[...] = assembled[:, NODE_DEV:]
    shift = pltpu.make_async_remote_copy(
        src_ref=next_buf, dst_ref=prev_buf, send_sem=shift_sems.at[0], recv_sem=shift_sems.at[1],
        device_id=following, device_id_type=MESH,
    )
    shift.start()
    for sent, arrival in returns:
        sent.wait_send()
    shift.wait()
    own = assembled[:, :NODE_DEV] + jnp.where(rank > 0, prev_buf[...], 0.0)
    force_ref[...] = own[:3]
    block_ref[...] = own[3:12]
    store.wait()


def tiled_body(
    strain, fiber_coeff, gradients, volume, corners, rve_worker, rve_slot, slot_element,
    state_table, loading, compliance,
):
    elem_rows = strain.shape[0]
    workers = lax.axis_size("rve")
    capacity = state_table.shape[0]
    nodes = compliance.shape[1]
    block = compliance.shape[0]
    rows = workers * ROW
    total = LOAD_PAD + 3 * SLOT_PAD
    vmem = pl.BlockSpec(memory_space=pltpu.VMEM)
    hbm = pl.BlockSpec(memory_space=pl.ANY)
    wide, narrow, whole = jnp.float32, jnp.bfloat16, jnp.int32
    dma = pltpu.SemaphoreType.DMA
    new_table, forces, blocks = pl.pallas_call(
        step_kernel,
        out_shape=(
            jax.ShapeDtypeStruct((3, capacity, nodes), wide),
            jax.ShapeDtypeStruct((3, NODE_DEV), wide),
            jax.ShapeDtypeStruct((9, NODE_DEV), wide),
        ),
        in_specs=[hbm] * 11, out_specs=(hbm, vmem, vmem),
        scratch_shapes=[
            pltpu.VMEM((6, elem_rows), narrow),
            pltpu.VMEM((elem_rows, nodes), narrow),
            pltpu.VMEM((12, elem_rows), wide),
            pltpu.VMEM((1, elem_rows), wide),
            pltpu.VMEM((4, elem_rows), whole),
            pltpu.VMEM((1, elem_rows), whole),
            pltpu.VMEM((1, elem_rows), whole),
            pltpu.VMEM((1, capacity), whole),
            pltpu.VMEM((3, capacity, nodes), wide),
            pltpu.VMEM((6, 3, nodes), narrow),
            pltpu.VMEM((block, block // 2), narrow),
            pltpu.VMEM((block // 2, block), narrow),
            pltpu.VMEM((rows, nodes + 128), narrow),
            pltpu.VMEM((workers, block, workers // 2 * block + block // 2), narrow),
            pltpu.VMEM((rows, nodes + 128), narrow),
            pltpu.VMEM((nodes, nodes), narrow),
            pltpu.VMEM((total, nodes), wide),
            pltpu.VMEM((SLOT_PAD, nodes), wide),
            pltpu.VMEM((total, nodes), wide),
            pltpu.VMEM((total, nodes), narrow),
            pltpu.VMEM((total, nodes), narrow),
            pltpu.VMEM((rows, 128), wide),
            pltpu.VMEM((rows, 128), wide),
            pltpu.VMEM((16, NODE_DEV), wide),
            pltpu.VMEM((16, NODE_DEV), wide),
            dma((workers // 2 + 13,)),
            dma((workers, 4, 5)),
            dma((workers, 4)),
            dma((workers,)),
            dma((workers,)),
            dma((workers,)),
            dma((workers,)),
            dma((2,)),
        ],
        compiler_params=pltpu.CompilerParams(
            vmem_limit_bytes=58 * 2**20, collective_id=0, has_side_effects=True
        ),
        name="step",
    )(
        strain.T, fiber_coeff, gradients, volume[None, :], corners, rve_worker[None, :],
        rve_slot[None, :], slot_element[None, :], jnp.transpose(state_table, (1, 0, 2)),
        loading, compliance,
    )
    return jnp.transpose(new_table, (1, 0, 2)), forces, blocks


def solution(mesh):
    def chosen(*args):
        workers, columns = lax.axis_size("rve"), lax.axis_size("blk")
        block = args[-1].shape[0]
        even = workers == 8 and columns == 4 and block % 256 == 0
        few = -(-args[8].shape[0] // workers) <= ROW and args[8].shape[0] <= SLOT_PAD
        return (tiled_body if even and few else body)(*args)

    return jax.shard_map(
        chosen,
        mesh=mesh,
        in_specs=(
            P(("rve", "blk"), None),
            P(("rve", "blk"), None),
            P(None, ("rve", "blk")),
            P(("rve", "blk")),
            P(None, ("rve", "blk")),
            P(("rve", "blk")),
            P(("rve", "blk")),
            P(("rve", "blk")),
            P(("rve", "blk"), None, None),
            P(),
            P("rve", None),
        ),
        out_specs=(P(("rve", "blk"), None, None), P(None, ("rve", "blk")), P(None, ("rve", "blk"))),
        check_vma=False,
    )
```

```python
import jax
import jax.numpy as jnp
import numpy as np
from jax import lax
from jax.experimental import pallas as pl
from jax.experimental.pallas import tpu as pltpu
from jax.sharding import PartitionSpec as P

ITERS = 3
NODE_DEV = 128


highest = lax.Precision.HIGHEST


def from_behind(block, axis, distance):
    devices = range(lax.axis_size(axis))
    route = [(i - distance, i) for i in devices if i - distance in devices]
    return lax.ppermute(block, axis, route)


def strain_map():
    voigt_map = np.zeros((6, 3, 3), np.float32)
    for voigt_row, first_axis, second_axis in (
        (0, 0, 0),
        (1, 1, 1),
        (2, 2, 2),
        (3, 1, 2),
        (3, 2, 1),
        (4, 0, 2),
        (4, 2, 0),
        (5, 0, 1),
        (5, 1, 0),
    ):
        voigt_map[voigt_row, first_axis, second_axis] = 1.0
    return jnp.asarray(voigt_map)


def micro_solve(strain_rows, coeff_rows, start_rows, loading, network, basis, fixed_part):
    batch_rows = strain_rows.shape[0]
    node_count = network.shape[0]
    mean_scale = 1.0 / (3 * node_count)
    forcing = jnp.dot(
        strain_rows, loading.reshape(6, 3 * node_count), preferred_element_type=jnp.float32
    ).reshape(batch_rows, 3, node_count)
    fiber_wide = coeff_rows[:, None, :].astype(jnp.float32)
    current = start_rows.reshape(batch_rows, 3, node_count)
    for iteration in range(ITERS):
        pressure = (
            (forcing - fiber_wide * jnp.tanh(current))
            .astype(jnp.bfloat16)
            .reshape(batch_rows * 3, node_count)
        )
        current = lax.dot_general(
            pressure, network, (((1,), (1,)), ((), ())), preferred_element_type=jnp.float32
        ).reshape(batch_rows, 3, node_count)
    flat_state = current.reshape(batch_rows, 3 * node_count)
    load_float = loading.reshape(6, 3 * node_count).astype(jnp.float32)
    stress = jnp.dot(flat_state, load_float.T, precision=highest) * mean_scale
    products = (basis[:, None, :] * basis[None, :, :]).reshape(36, 3 * node_count)
    damping = (fiber_wide * (1.0 - jnp.tanh(current) ** 2)).reshape(batch_rows, 3 * node_count)
    tangent = (
        fixed_part.reshape(1, 36) - jnp.dot(damping, products.T, precision=highest)
    ) * mean_scale
    return (flat_state, stress, tangent)


def body(
    strain,
    fiber_coeff,
    gradients,
    volume,
    corners,
    rve_worker,
    rve_slot,
    slot_element,
    state_table,
    loading,
    compliance,
):
    elem_rows = strain.shape[0]
    workers = lax.axis_size("rve")
    columns = lax.axis_size("blk")
    capacity = state_table.shape[0]
    slot_cap = (capacity + workers - 1) // workers
    node_count = compliance.shape[1]
    buffer_rows = workers * slot_cap
    network = lax.all_gather(compliance, "rve", axis=0, tiled=True)
    basis = lax.dot_general(
        loading.reshape(18, node_count),
        network,
        (((1,), (1,)), ((), ())),
        preferred_element_type=jnp.float32,
    ).reshape(6, 3 * node_count)
    fixed_part = jnp.dot(
        loading.reshape(6, 3 * node_count).astype(jnp.float32), basis.T, precision=highest
    )
    earlier = (rve_worker[None, :] == rve_worker[:, None]) & (rve_slot[None, :] < rve_slot[:, None])
    home_pos = rve_worker * slot_cap + jnp.sum(earlier, axis=1)
    occupied = slot_element >= 0
    source_home = jnp.where(occupied, slot_element // elem_rows // columns, -1)
    slot_ids = jnp.arange(capacity)
    before = (source_home[None, :] == source_home[:, None]) & (
        slot_ids[None, :] < slot_ids[:, None]
    )
    work_pos = jnp.where(occupied, source_home * slot_cap + jnp.sum(before, axis=1), buffer_rows)
    fetch_pos = jnp.minimum(work_pos, buffer_rows - 1)
    flat_table = state_table.reshape(capacity, 3 * node_count)
    send_strain = jnp.zeros((buffer_rows, 6), jnp.bfloat16).at[home_pos].set(strain)
    send_coeff = jnp.zeros((buffer_rows, node_count), jnp.bfloat16).at[home_pos].set(fiber_coeff)
    got_strain, got_coeff = (
        lax.all_to_all(
            send_strain.reshape(workers, slot_cap, 6),
            "rve",
            split_axis=0,
            concat_axis=0,
            tiled=True,
        ),
        lax.all_to_all(
            send_coeff.reshape(workers, slot_cap, node_count),
            "rve",
            split_axis=0,
            concat_axis=0,
            tiled=True,
        ),
    )
    slot_strain = jnp.where(occupied[:, None], got_strain.reshape(buffer_rows, 6)[fetch_pos], 0)
    slot_coeff = jnp.where(
        occupied[:, None], got_coeff.reshape(buffer_rows, node_count)[fetch_pos], 0
    )
    finals, slot_stress, slot_tangent = micro_solve(
        slot_strain, slot_coeff, flat_table, loading, network, basis, fixed_part
    )
    new_table = jnp.where(occupied[:, None], finals, flat_table)
    back_stress = (
        jnp.zeros((buffer_rows, 6), jnp.float32).at[work_pos].set(slot_stress, mode="drop")
    )
    back_tangent = (
        jnp.zeros((buffer_rows, 36), jnp.float32).at[work_pos].set(slot_tangent, mode="drop")
    )
    ret_stress, ret_tangent = (
        lax.all_to_all(
            back_stress.reshape(workers, slot_cap, 6),
            "rve",
            split_axis=0,
            concat_axis=0,
            tiled=True,
        ),
        lax.all_to_all(
            back_tangent.reshape(workers, slot_cap, 36),
            "rve",
            split_axis=0,
            concat_axis=0,
            tiled=True,
        ),
    )
    stress = ret_stress.reshape(buffer_rows, 6)[home_pos]
    tangent = ret_tangent.reshape(buffer_rows, 36)[home_pos]
    gradient_rows = gradients.reshape(4, 3, elem_rows)
    bmatrix = jnp.einsum("vac,ich->ivah", strain_map(), gradient_rows, precision=highest)
    corner_force = volume * jnp.einsum("ivah,hv->iah", bmatrix, stress, precision=highest)
    corner_block = volume * jnp.einsum(
        "ivah,hvw,iwbh->iabh", bmatrix, tangent.reshape(elem_rows, 6, 6), bmatrix, precision=highest
    )
    contrib = jnp.concatenate([corner_force, corner_block.reshape(4, 9, elem_rows)], axis=1)
    contrib = jnp.transpose(contrib, (1, 0, 2)).reshape(12, 4 * elem_rows)
    device_rank = lax.axis_index("rve") * columns + lax.axis_index("blk")
    local_node = (corners - device_rank * NODE_DEV).reshape(4 * elem_rows)
    onehot = (local_node[:, None] == jnp.arange(2 * NODE_DEV)[None, :]).astype(jnp.float32)
    assembled = jnp.dot(contrib, onehot, precision=highest)
    own_rows = assembled[:, :NODE_DEV] + from_behind(assembled[:, NODE_DEV:], ("rve", "blk"), 1)
    return (new_table.reshape(capacity, 3, node_count), own_rows[:3], own_rows[3:])


ROW = 16
PARTS = 2
SLOT_PAD = 88
LOAD_PAD = 24


def to_column(row):
    count = row.shape[1]
    grid_row = lax.broadcasted_iota(jnp.int32, (count, count), 0)
    grid_col = lax.broadcasted_iota(jnp.int32, (count, count), 1)
    return jnp.sum(jnp.where(grid_row == grid_col, row, 0), axis=1, keepdims=True)


def home_positions(worker_row, slot_row, slots):
    same = to_column(worker_row) == worker_row
    ahead = to_column(slot_row) < slot_row
    rank = jnp.sum(jnp.where(same & ahead, 1, 0), axis=0, keepdims=True)
    return worker_row * slots + rank


def home_onehot(worker_row, slot_row, rows):
    positions = home_positions(worker_row, slot_row, ROW)
    row_ids = lax.broadcasted_iota(jnp.int32, (rows, positions.shape[1]), 0)
    return (row_ids == positions).astype(jnp.float32)


def work_positions(source_row, slots):
    count = source_row.shape[1]
    slot_ids = lax.broadcasted_iota(jnp.int32, (count, count), 0)
    later_ids = lax.broadcasted_iota(jnp.int32, (count, count), 1)
    same = to_column(source_row) == source_row
    rank = jnp.sum(jnp.where(same & (slot_ids < later_ids), 1, 0), axis=0, keepdims=True)
    shifted = jnp.where(source_row >= 0, source_row * slots + rank + 2, 0)
    grid_row = lax.broadcasted_iota(jnp.int32, (SLOT_PAD, count), 0)
    grid_col = lax.broadcasted_iota(jnp.int32, (SLOT_PAD, count), 1)
    return jnp.sum(jnp.where(grid_row == grid_col, shifted, 0), axis=1, keepdims=True) - 2


def folded_positions(row_ids, fold, tile, slots):
    inside = fold * ROW + (row_ids & (ROW - 1)) - tile * slots
    target = (row_ids >> 4) * slots + inside
    return jnp.where((inside >= 0) & (inside < slots), target, -1)


def dot_nt(left, right, **kwargs):
    return lax.dot_general(
        left, right, (((1,), (1,)), ((), ())), preferred_element_type=jnp.float32, **kwargs
    )


def dot_tn(left, right, **kwargs):
    return lax.dot_general(
        left, right, (((0,), (0,)), ((), ())), preferred_element_type=jnp.float32, **kwargs
    )


def split_wide(values):
    high = values.astype(jnp.bfloat16)
    return high, (values - high.astype(jnp.float32)).astype(jnp.bfloat16)


MESH = pl.DeviceIdType.MESH


def greet(targets):
    barrier = pltpu.get_barrier_semaphore()
    for device in targets:
        pl.semaphore_signal(barrier, inc=1, device_id=device, device_id_type=MESH)
    pl.semaphore_wait(barrier, len(targets))


def exchange(send_ref, recv_ref, send_sems, recv_sems, me, workers):
    copies = []
    for offset in range(1, workers):
        peer = lax.rem(me + offset, workers)
        source = lax.rem(me + workers - offset, workers)
        sent = pltpu.make_async_remote_copy(
            src_ref=send_ref.at[pl.ds(pl.multiple_of(peer * ROW, ROW), ROW)],
            dst_ref=recv_ref.at[pl.ds(pl.multiple_of(me * ROW, ROW), ROW)],
            send_sem=send_sems.at[peer],
            recv_sem=recv_sems.at[me],
            device_id={"rve": peer},
            device_id_type=MESH,
        )
        sent.start()
        landing = recv_ref.at[pl.ds(pl.multiple_of(source * ROW, ROW), ROW)]
        arrival = pltpu.make_async_remote_copy(
            src_ref=landing,
            dst_ref=landing,
            send_sem=send_sems.at[peer],
            recv_sem=recv_sems.at[source],
            device_id={"rve": peer},
            device_id_type=MESH,
        )
        copies.append((sent, arrival))
    here = pl.ds(pl.multiple_of(me * ROW, ROW), ROW)
    recv_ref[here, :] = send_ref[here, :]
    return copies


def step_kernel(
    strain_hbm, fiber_hbm, gradient_hbm, volume_hbm, corner_hbm, worker_hbm, slot_hbm, element_hbm,
    state_hbm, loading_hbm, compliance_hbm, new_hbm, force_ref, block_ref,
    strain_ref, fiber_ref, gradient_ref, volume_ref, corner_ref, worker_ref, slot_ref, element_ref,
    state_ref, loading_ref, left_ref, lower_ref, got_ref, net_ref, send_buf,
    dense, forcing, coeff, current, pressure_a, pressure_b, back_ref, ret_ref, next_buf, prev_buf,
    load_sems, net_send, net_recv, coeff_send, coeff_recv, ret_send, ret_recv, shift_sems
):
    workers, block, width = net_ref.shape
    columns = lax.axis_size("blk")
    near = workers // 2
    piece_rows = block // (4 * PARTS)
    nodes = compliance_hbm.shape[1]
    elem_rows = fiber_hbm.shape[0]
    capacity = state_hbm.shape[1]
    rows = send_buf.shape[0]
    mean_scale = 1.0 / (3 * nodes)
    me = lax.axis_index("rve")
    lane = lax.axis_index("blk")
    z, y = me // 2, lax.rem(me, 2)
    x, core = lane // 2, lax.rem(lane, 2)
    rank = me * columns + lane
    ahead = lax.rem(rank + 1, workers * columns)
    behind = lax.rem(rank + workers * columns - 1, workers * columns)
    following = {"rve": ahead // columns, "blk": lax.rem(ahead, columns)}
    leading = {"rve": behind // columns, "blk": lax.rem(behind, columns)}
    routes = (
        {"rve": me + 2},
        {"rve": me - 2},
        {"rve": me + 1 - 2 * y},
        {"blk": lane + 2 - 4 * x},
        {"blk": lane + 1 - 2 * core},
    )
    up, down, across, over, twin = range(5)
    far = pl.multiple_of(lax.rem(me + near, workers) * block, block)
    own_slab = []
    for step in range(near):
        column = pl.multiple_of(lax.rem(me + step, workers) * block, block)
        own_slab.append((
            compliance_hbm.at[:, pl.ds(column, block)],
            net_ref.at[me, :, pl.ds(step * block, block)],
        ))
    own_slab += [
        (compliance_hbm.at[:, pl.ds(far, block // 2)], left_ref),
        (compliance_hbm.at[pl.ds(block // 2, block // 2), pl.ds(far, block)], lower_ref),
    ]
    packs = [
        (strain_hbm, strain_ref), (fiber_hbm, fiber_ref), (worker_hbm, worker_ref),
        (slot_hbm, slot_ref),
    ]
    laters = [
        (element_hbm, element_ref), (loading_hbm, loading_ref), (state_hbm, state_ref),
        (gradient_hbm, gradient_ref), (volume_hbm, volume_ref), (corner_hbm, corner_ref),
    ]
    loads = [
        pltpu.make_async_copy(src, dst, load_sems.at[at])
        for at, (src, dst) in enumerate(own_slab + packs + laters)
    ]
    for load in loads:
        load.start()
    slab_loads, pack_loads = loads[:len(own_slab)], loads[len(own_slab):len(own_slab) + len(packs)]
    later_loads = loads[len(own_slab) + len(packs):]
    greet(
        [{"rve": lax.rem(me + offset, workers)} for offset in range(1, workers)]
        + [routes[over], routes[twin], following, leading]
    )
    for load in slab_loads:
        load.wait()
    net_ref[me, :, near * block:] = jnp.where(me < near, left_ref[...], lower_ref[...].T)

    def copy(owner, q, route):
        piece = net_ref.at[owner, pl.ds(pl.multiple_of(q * piece_rows, piece_rows), piece_rows)]
        return pltpu.make_async_remote_copy(
            src_ref=piece,
            dst_ref=piece,
            send_sem=net_send.at[owner, q, route],
            recv_sem=net_recv.at[owner, q],
            device_id=routes[route],
            device_id_type=MESH,
        )

    sends = []

    def push(cond, owner, q, route):
        sends.append((cond, owner, q, route))
        if cond is True:
            copy(owner, q, route).start()
        else:
            pl.when(cond)(lambda: copy(owner, q, route).start())

    def arrive(cond, owner, q):
        if cond is True:
            copy(owner, q, twin).wait_recv()
        else:
            pl.when(cond)(lambda: copy(owner, q, twin).wait_recv())

    k, k2 = 2 * core + x, 2 * core + 1 - x
    has_up, has_down = z < near - 1, z > 0
    def parts(q):
        return [q * PARTS + part for part in range(PARTS)]

    for q in parts(k):
        push(has_up, me, q, up)
        push(has_down, me, q, down)
        push(True, me, q, across)
    for q in parts(k2):
        push(has_up, me, q, up)
        push(has_down, me, q, down)
    for load in pack_loads:
        load.wait()
    home = home_onehot(worker_ref[...], slot_ref[...], rows)
    slots_each = (capacity + workers - 1) // workers
    tiles = nodes // 128 + 1
    home_at = home_positions(worker_ref[...], slot_ref[...], slots_each)
    row_ids = lax.broadcasted_iota(jnp.int32, (rows, elem_rows), 0)
    for fold in range(send_buf.shape[1] // 128):
        packed = jnp.zeros((rows, 128), jnp.float32)
        for tile in range(fold * ROW // slots_each, (fold * ROW + ROW - 1) // slots_each + 1):
            target = folded_positions(row_ids, fold, tile, slots_each)
            picked = (target == home_at).astype(jnp.bfloat16)
            if tile < tiles - 1:
                packed += jnp.dot(
                    picked, fiber_ref[:, tile * 128:(tile + 1) * 128],
                    preferred_element_type=jnp.float32,
                )
            elif tile == tiles - 1:
                packed += jnp.concatenate(
                    [dot_nt(picked, strain_ref[...]), jnp.zeros((rows, 122), jnp.float32)], axis=1
                )
        send_buf[:, fold * 128:(fold + 1) * 128] = packed.astype(jnp.bfloat16)
    copies = exchange(send_buf, got_ref, coeff_send, coeff_recv, me, workers)

    def lines(distance):
        if distance == 0:
            return [(True, me, None, None)]
        return [
            (z >= distance, me - 2 * distance, up, has_up),
            (z < near - distance, me + 2 * distance, down, has_down),
        ]

    def from_across(distance):
        for has, owner, route, edge in lines(distance):
            other = owner + 1 - 2 * y
            for q in parts(k):
                arrive(has, other, q)
                push(has, other, q, over)
                push(has, other, q, twin)

    def from_over(distance):
        for has, owner, route, edge in lines(distance):
            other = owner + 1 - 2 * y
            for q in parts(k2):
                arrive(has, other, q)
                push(has, other, q, twin)

    def place(owner):
        rows_here = pl.ds(pl.multiple_of(owner * block, block), block)
        for step in range(near):
            there = pl.ds(pl.multiple_of(lax.rem(owner + step, workers) * block, block), block)
            tile = net_ref[owner, :, step * block:(step + 1) * block]
            dense[rows_here, there] = tile
            if step:
                dense[there, rows_here] = tile.T
        tile = net_ref[owner, :, near * block:]
        low = owner < near
        row = pl.multiple_of(jnp.where(low, owner, owner - near) * block, block)
        half = block // 2
        column = pl.multiple_of(jnp.where(low, (owner + near) * block, owner * block + half), half)
        dense[pl.ds(row, block), pl.ds(column, half)] = tile
        dense[pl.ds(column, half), pl.ds(row, block)] = tile.T

    def finish(z_other, y_other):
        owner = z_other * 2 + y_other
        for q in parts(2 - 2 * core) + parts(3 - 2 * core):
            arrive(True, owner, q)
        place(owner)

    def setup():
        for load in later_loads:
            load.wait()
        for sent, arrival in copies:
            arrival.wait_recv()
        element_row = element_ref[...]
        source = jnp.full(element_row.shape, -1, jnp.int32)
        for worker in range(workers):
            source += jnp.where(element_row >= worker * elem_rows * columns, 1, 0)
        lane_at = lax.broadcasted_iota(jnp.int32, (SLOT_PAD, rows), 1)
        onehot = (lane_at == work_positions(source, ROW)).astype(jnp.float32)
        work_at = work_positions(source, slots_each)
        for tile in range(tiles):
            wanted = jnp.zeros((SLOT_PAD, 128), jnp.float32)
            first, final = tile * slots_each // ROW, (tile * slots_each + slots_each - 1) // ROW
            for fold in range(first, final + 1):
                target = folded_positions(lane_at, fold, tile, slots_each)
                wanted += jnp.dot(
                    (target == work_at).astype(jnp.bfloat16),
                    got_ref[:, fold * 128:(fold + 1) * 128],
                    preferred_element_type=jnp.float32,
                )
            if tile < tiles - 1:
                coeff[:, tile * 128:(tile + 1) * 128] = wanted
        strain_rows = wanted[:, :8].astype(jnp.bfloat16)
        forcing[0:LOAD_PAD, :] = jnp.zeros((LOAD_PAD, nodes), jnp.float32)
        for k_load in range(6):
            three = loading_ref[k_load].astype(jnp.float32)
            for axis in range(3):
                forcing[axis * 8 + k_load:axis * 8 + k_load + 1, :] = three[axis:axis + 1, :]
        current[0:LOAD_PAD, :] = jnp.zeros((LOAD_PAD, nodes), jnp.float32)
        for axis in range(3):
            start = LOAD_PAD + axis * SLOT_PAD
            load_rows = forcing[axis * 8:axis * 8 + 8, :].astype(jnp.bfloat16)
            forcing[start:start + SLOT_PAD, :] = jnp.dot(
                strain_rows, load_rows, preferred_element_type=jnp.float32
            )
            current[start + 80:start + SLOT_PAD, :] = jnp.zeros((SLOT_PAD - 80, nodes), jnp.float32)
            current[start:start + capacity, :] = state_ref[axis]
        for tile in range(nodes // block):
            lanes = slice(tile * block, (tile + 1) * block)
            pressure_a[:, lanes] = press(current[:, lanes], lanes)
        return onehot

    def press(values, lanes):
        c = coeff[:, lanes]
        wide = jnp.concatenate([jnp.zeros((LOAD_PAD, c.shape[1]), jnp.float32), c, c, c], axis=0)
        return (forcing[:, lanes] - wide * jnp.tanh(values)).astype(jnp.bfloat16)

    last = near - 1
    full = 1
    z_one = z + 1 - 2 * lax.rem(z, 2)
    z_two = lax.rem(z + 2, near)
    z_three = last - z

    def from_over_line(distance):
        for has, owner, route, edge in lines(distance):
            for q in parts(k2):
                arrive(has, owner, q)
                push(has, owner, q, twin)

    from_across(0)
    for distance in range(1, near):
        for has, owner, route, edge in lines(distance):
            for q in parts(k):
                arrive(has, owner, q)
                if distance < last:
                    push(has & edge, owner, q, route)
                push(has, owner, q, across)
                if distance > full:
                    push(has, owner, q, over)
                push(has, owner, q, twin)
        if distance <= full:
            for has, owner, route, edge in lines(distance):
                for q in parts(k2):
                    arrive(has, owner, q)
                    if distance + 1 <= full:
                        push(has & edge, owner, q, route)
                    push(has, owner, q, twin)
        from_over(distance - 1)
        if distance - 1 > full:
            from_over_line(distance - 1)
        from_across(distance)
        if distance == 2:
            place(me)
            finish(z, 1 - y)
    onehot = setup()
    finish(z_one, y)
    from_over_line(last)
    from_over(last)
    finish(z_one, 1 - y)
    for z_other in (z_two, z_three):
        finish(z_other, y)
        finish(z_other, 1 - y)

    for iteration in range(ITERS):
        reads, writes = (pressure_a, pressure_b) if iteration % 2 == 0 else (pressure_b, pressure_a)
        for tile in range(nodes // block):
            lanes = slice(tile * block, (tile + 1) * block)
            values = jnp.dot(reads[...], dense[:, lanes], preferred_element_type=jnp.float32)
            if iteration == ITERS - 1:
                current[:, lanes] = values
            else:
                writes[:, lanes] = press(values, lanes)

    occupied = jnp.sum(onehot, axis=1, keepdims=True) > 0.5
    tangent = jnp.zeros((SLOT_PAD, 96), jnp.float32)
    tangent_low = jnp.zeros((SLOT_PAD, 48), jnp.float32)
    stress = jnp.zeros((SLOT_PAD, 8), jnp.float32)
    fixed = jnp.zeros((8, 8), jnp.float32)
    for axis in range(3):
        start = LOAD_PAD + axis * SLOT_PAD
        final = current[start:start + SLOT_PAD, :]
        state_ref[axis] = jnp.where(
            occupied[:capacity], current[start:start + capacity, :], state_ref[axis]
        )
        basis = current[axis * 8:axis * 8 + 8, :]
        load = forcing[axis * 8:axis * 8 + 8, :].astype(jnp.bfloat16)
        products = jnp.concatenate([basis[k:k + 1, :] * basis for k in range(6)], axis=0)
        products_high, products_low = split_wide(products)
        damping = coeff[...] * (1.0 - jnp.tanh(final) ** 2)
        damping_high, damping_low = split_wide(damping)
        tangent += dot_nt(damping_high, jnp.concatenate([products_high, products_low], axis=0))
        tangent_low += dot_nt(damping_low, products_high)
        final_high, final_low = split_wide(final)
        stress += dot_nt(final_high, load) + dot_nt(final_low, load)
        basis_high, basis_low = split_wide(basis)
        fixed += dot_nt(load, basis_high) + dot_nt(load, basis_low)
    store = pltpu.make_async_copy(state_ref, new_hbm, load_sems.at[len(loads)])
    store.start()
    lane_ids = lax.broadcasted_iota(jnp.int32, (8, 48), 1)
    row_ids = lax.broadcasted_iota(jnp.int32, (8, 48), 0)
    spread = jnp.dot(
        fixed, (lane_ids % 8 == row_ids).astype(jnp.float32), precision=highest,
        preferred_element_type=jnp.float32,
    )
    fixed_row = jnp.sum(jnp.where(lane_ids // 8 == row_ids, spread, 0.0), axis=0, keepdims=True)
    total = fixed_row - (tangent[:, :48] + tangent[:, 48:] + tangent_low)
    packed = jnp.concatenate(
        [total, stress, jnp.zeros((SLOT_PAD, 72), jnp.float32)], axis=1
    ) * mean_scale
    back_ref[...] = dot_tn(onehot, packed, precision=highest)
    returns = exchange(back_ref, ret_ref, ret_send, ret_recv, me, workers)
    for sent, arrival in copies:
        sent.wait_send()
    for cond, owner, q, route in sends:
        if cond is True:
            copy(owner, q, route).wait_send()
        else:
            pl.when(cond)(lambda: copy(owner, q, route).wait_send())
    for sent, arrival in returns:
        arrival.wait_recv()
    values = dot_tn(ret_ref[...], home, precision=highest)
    volume = volume_ref[...]
    count = volume.shape[1]
    stress = [values[48 + k:49 + k, :] for k in range(6)]
    rows_of = [values[k * 8:k * 8 + 8, :] for k in range(6)]
    node_ids = lax.broadcasted_iota(jnp.int32, (2 * NODE_DEV, count), 0)
    assembled = jnp.zeros((16, 2 * NODE_DEV), jnp.float32)

    def apply(g, terms):
        gx, gy, gz = g
        return (
            gx * terms[0] + gz * terms[4] + gy * terms[5],
            gy * terms[1] + gz * terms[3] + gx * terms[5],
            gz * terms[2] + gy * terms[3] + gx * terms[4],
        )

    for corner in range(4):
        g = [gradient_ref[3 * corner + c:3 * corner + c + 1, :] for c in range(3)]
        lines = [volume * f for f in apply(g, stress)]
        for u in apply(g, rows_of):
            lines += [volume * m for m in apply(g, [u[j:j + 1, :] for j in range(6)])]
        contrib = jnp.concatenate(lines + [jnp.zeros((4, count), jnp.float32)], axis=0)
        picked = (node_ids == corner_ref[corner:corner + 1, :] - rank * NODE_DEV).astype(jnp.float32)
        assembled += dot_nt(contrib, picked, precision=highest)
    next_buf[...] = assembled[:, NODE_DEV:]
    shift = pltpu.make_async_remote_copy(
        src_ref=next_buf, dst_ref=prev_buf, send_sem=shift_sems.at[0], recv_sem=shift_sems.at[1],
        device_id=following, device_id_type=MESH,
    )
    shift.start()
    for sent, arrival in returns:
        sent.wait_send()
    shift.wait()
    own = assembled[:, :NODE_DEV] + jnp.where(rank > 0, prev_buf[...], 0.0)
    force_ref[...] = own[:3]
    block_ref[...] = own[3:12]
    store.wait()


def tiled_body(
    strain, fiber_coeff, gradients, volume, corners, rve_worker, rve_slot, slot_element,
    state_table, loading, compliance,
):
    elem_rows = strain.shape[0]
    workers = lax.axis_size("rve")
    capacity = state_table.shape[0]
    nodes = compliance.shape[1]
    block = compliance.shape[0]
    rows = workers * ROW
    total = LOAD_PAD + 3 * SLOT_PAD
    slots_each = (capacity + workers - 1) // workers
    folded = ((nodes // 128 + 1) * slots_each + ROW - 1) // ROW
    vmem = pl.BlockSpec(memory_space=pltpu.VMEM)
    hbm = pl.BlockSpec(memory_space=pl.ANY)
    wide, narrow, whole = jnp.float32, jnp.bfloat16, jnp.int32
    dma = pltpu.SemaphoreType.DMA
    new_table, forces, blocks = pl.pallas_call(
        step_kernel,
        out_shape=(
            jax.ShapeDtypeStruct((3, capacity, nodes), wide),
            jax.ShapeDtypeStruct((3, NODE_DEV), wide),
            jax.ShapeDtypeStruct((9, NODE_DEV), wide),
        ),
        in_specs=[hbm] * 11, out_specs=(hbm, vmem, vmem),
        scratch_shapes=[
            pltpu.VMEM((6, elem_rows), narrow),
            pltpu.VMEM((elem_rows, nodes), narrow),
            pltpu.VMEM((12, elem_rows), wide),
            pltpu.VMEM((1, elem_rows), wide),
            pltpu.VMEM((4, elem_rows), whole),
            pltpu.VMEM((1, elem_rows), whole),
            pltpu.VMEM((1, elem_rows), whole),
            pltpu.VMEM((1, capacity), whole),
            pltpu.VMEM((3, capacity, nodes), wide),
            pltpu.VMEM((6, 3, nodes), narrow),
            pltpu.VMEM((block, block // 2), narrow),
            pltpu.VMEM((block // 2, block), narrow),
            pltpu.VMEM((rows, folded * 128), narrow),
            pltpu.VMEM((workers, block, workers // 2 * block + block // 2), narrow),
            pltpu.VMEM((rows, folded * 128), narrow),
            pltpu.VMEM((nodes, nodes), narrow),
            pltpu.VMEM((total, nodes), wide),
            pltpu.VMEM((SLOT_PAD, nodes), wide),
            pltpu.VMEM((total, nodes), wide),
            pltpu.VMEM((total, nodes), narrow),
            pltpu.VMEM((total, nodes), narrow),
            pltpu.VMEM((rows, 128), wide),
            pltpu.VMEM((rows, 128), wide),
            pltpu.VMEM((16, NODE_DEV), wide),
            pltpu.VMEM((16, NODE_DEV), wide),
            dma((workers // 2 + 13,)),
            dma((workers, 4 * PARTS, 5)),
            dma((workers, 4 * PARTS)),
            dma((workers,)),
            dma((workers,)),
            dma((workers,)),
            dma((workers,)),
            dma((2,)),
        ],
        compiler_params=pltpu.CompilerParams(
            vmem_limit_bytes=58 * 2**20, collective_id=0, has_side_effects=True
        ),
        name="step",
    )(
        strain.T, fiber_coeff, gradients, volume[None, :], corners, rve_worker[None, :],
        rve_slot[None, :], slot_element[None, :], jnp.transpose(state_table, (1, 0, 2)),
        loading, compliance,
    )
    return jnp.transpose(new_table, (1, 0, 2)), forces, blocks


def solution(mesh):
    def chosen(*args):
        workers, columns = lax.axis_size("rve"), lax.axis_size("blk")
        block = args[-1].shape[0]
        even = workers == 8 and columns == 4 and block % 256 == 0
        few = -(-args[8].shape[0] // workers) <= ROW and args[8].shape[0] <= SLOT_PAD
        return (tiled_body if even and few else body)(*args)

    return jax.shard_map(
        chosen,
        mesh=mesh,
        in_specs=(
            P(("rve", "blk"), None),
            P(("rve", "blk"), None),
            P(None, ("rve", "blk")),
            P(("rve", "blk")),
            P(None, ("rve", "blk")),
            P(("rve", "blk")),
            P(("rve", "blk")),
            P(("rve", "blk")),
            P(("rve", "blk"), None, None),
            P(),
            P("rve", None),
        ),
        out_specs=(P(("rve", "blk"), None, None), P(None, ("rve", "blk")), P(None, ("rve", "blk"))),
        check_vma=False,
    )
```

```python
import jax
import jax.numpy as jnp
import numpy as np
from jax import lax
from jax.experimental import pallas as pl
from jax.experimental.pallas import tpu as pltpu
from jax.sharding import PartitionSpec as P

ITERS = 3
NODE_DEV = 128


highest = lax.Precision.HIGHEST


def from_behind(block, axis, distance):
    devices = range(lax.axis_size(axis))
    route = [(i - distance, i) for i in devices if i - distance in devices]
    return lax.ppermute(block, axis, route)


def strain_map():
    voigt_map = np.zeros((6, 3, 3), np.float32)
    for voigt_row, first_axis, second_axis in (
        (0, 0, 0),
        (1, 1, 1),
        (2, 2, 2),
        (3, 1, 2),
        (3, 2, 1),
        (4, 0, 2),
        (4, 2, 0),
        (5, 0, 1),
        (5, 1, 0),
    ):
        voigt_map[voigt_row, first_axis, second_axis] = 1.0
    return jnp.asarray(voigt_map)


def micro_solve(strain_rows, coeff_rows, start_rows, loading, network, basis, fixed_part):
    batch_rows = strain_rows.shape[0]
    node_count = network.shape[0]
    mean_scale = 1.0 / (3 * node_count)
    forcing = jnp.dot(
        strain_rows, loading.reshape(6, 3 * node_count), preferred_element_type=jnp.float32
    ).reshape(batch_rows, 3, node_count)
    fiber_wide = coeff_rows[:, None, :].astype(jnp.float32)
    current = start_rows.reshape(batch_rows, 3, node_count)
    for iteration in range(ITERS):
        pressure = (
            (forcing - fiber_wide * jnp.tanh(current))
            .astype(jnp.bfloat16)
            .reshape(batch_rows * 3, node_count)
        )
        current = lax.dot_general(
            pressure, network, (((1,), (1,)), ((), ())), preferred_element_type=jnp.float32
        ).reshape(batch_rows, 3, node_count)
    flat_state = current.reshape(batch_rows, 3 * node_count)
    load_float = loading.reshape(6, 3 * node_count).astype(jnp.float32)
    stress = jnp.dot(flat_state, load_float.T, precision=highest) * mean_scale
    products = (basis[:, None, :] * basis[None, :, :]).reshape(36, 3 * node_count)
    damping = (fiber_wide * (1.0 - jnp.tanh(current) ** 2)).reshape(batch_rows, 3 * node_count)
    tangent = (
        fixed_part.reshape(1, 36) - jnp.dot(damping, products.T, precision=highest)
    ) * mean_scale
    return (flat_state, stress, tangent)


def body(
    strain,
    fiber_coeff,
    gradients,
    volume,
    corners,
    rve_worker,
    rve_slot,
    slot_element,
    state_table,
    loading,
    compliance,
):
    elem_rows = strain.shape[0]
    workers = lax.axis_size("rve")
    columns = lax.axis_size("blk")
    capacity = state_table.shape[0]
    slot_cap = (capacity + workers - 1) // workers
    node_count = compliance.shape[1]
    buffer_rows = workers * slot_cap
    network = lax.all_gather(compliance, "rve", axis=0, tiled=True)
    basis = lax.dot_general(
        loading.reshape(18, node_count),
        network,
        (((1,), (1,)), ((), ())),
        preferred_element_type=jnp.float32,
    ).reshape(6, 3 * node_count)
    fixed_part = jnp.dot(
        loading.reshape(6, 3 * node_count).astype(jnp.float32), basis.T, precision=highest
    )
    earlier = (rve_worker[None, :] == rve_worker[:, None]) & (rve_slot[None, :] < rve_slot[:, None])
    home_pos = rve_worker * slot_cap + jnp.sum(earlier, axis=1)
    occupied = slot_element >= 0
    source_home = jnp.where(occupied, slot_element // elem_rows // columns, -1)
    slot_ids = jnp.arange(capacity)
    before = (source_home[None, :] == source_home[:, None]) & (
        slot_ids[None, :] < slot_ids[:, None]
    )
    work_pos = jnp.where(occupied, source_home * slot_cap + jnp.sum(before, axis=1), buffer_rows)
    fetch_pos = jnp.minimum(work_pos, buffer_rows - 1)
    flat_table = state_table.reshape(capacity, 3 * node_count)
    send_strain = jnp.zeros((buffer_rows, 6), jnp.bfloat16).at[home_pos].set(strain)
    send_coeff = jnp.zeros((buffer_rows, node_count), jnp.bfloat16).at[home_pos].set(fiber_coeff)
    got_strain, got_coeff = (
        lax.all_to_all(
            send_strain.reshape(workers, slot_cap, 6),
            "rve",
            split_axis=0,
            concat_axis=0,
            tiled=True,
        ),
        lax.all_to_all(
            send_coeff.reshape(workers, slot_cap, node_count),
            "rve",
            split_axis=0,
            concat_axis=0,
            tiled=True,
        ),
    )
    slot_strain = jnp.where(occupied[:, None], got_strain.reshape(buffer_rows, 6)[fetch_pos], 0)
    slot_coeff = jnp.where(
        occupied[:, None], got_coeff.reshape(buffer_rows, node_count)[fetch_pos], 0
    )
    finals, slot_stress, slot_tangent = micro_solve(
        slot_strain, slot_coeff, flat_table, loading, network, basis, fixed_part
    )
    new_table = jnp.where(occupied[:, None], finals, flat_table)
    back_stress = (
        jnp.zeros((buffer_rows, 6), jnp.float32).at[work_pos].set(slot_stress, mode="drop")
    )
    back_tangent = (
        jnp.zeros((buffer_rows, 36), jnp.float32).at[work_pos].set(slot_tangent, mode="drop")
    )
    ret_stress, ret_tangent = (
        lax.all_to_all(
            back_stress.reshape(workers, slot_cap, 6),
            "rve",
            split_axis=0,
            concat_axis=0,
            tiled=True,
        ),
        lax.all_to_all(
            back_tangent.reshape(workers, slot_cap, 36),
            "rve",
            split_axis=0,
            concat_axis=0,
            tiled=True,
        ),
    )
    stress = ret_stress.reshape(buffer_rows, 6)[home_pos]
    tangent = ret_tangent.reshape(buffer_rows, 36)[home_pos]
    gradient_rows = gradients.reshape(4, 3, elem_rows)
    bmatrix = jnp.einsum("vac,ich->ivah", strain_map(), gradient_rows, precision=highest)
    corner_force = volume * jnp.einsum("ivah,hv->iah", bmatrix, stress, precision=highest)
    corner_block = volume * jnp.einsum(
        "ivah,hvw,iwbh->iabh", bmatrix, tangent.reshape(elem_rows, 6, 6), bmatrix, precision=highest
    )
    contrib = jnp.concatenate([corner_force, corner_block.reshape(4, 9, elem_rows)], axis=1)
    contrib = jnp.transpose(contrib, (1, 0, 2)).reshape(12, 4 * elem_rows)
    device_rank = lax.axis_index("rve") * columns + lax.axis_index("blk")
    local_node = (corners - device_rank * NODE_DEV).reshape(4 * elem_rows)
    onehot = (local_node[:, None] == jnp.arange(2 * NODE_DEV)[None, :]).astype(jnp.float32)
    assembled = jnp.dot(contrib, onehot, precision=highest)
    own_rows = assembled[:, :NODE_DEV] + from_behind(assembled[:, NODE_DEV:], ("rve", "blk"), 1)
    return (new_table.reshape(capacity, 3, node_count), own_rows[:3], own_rows[3:])


ROW = 16
PARTS = 2
SLOT_PAD = 88
LOAD_PAD = 24


def to_column(row):
    count = row.shape[1]
    grid_row = lax.broadcasted_iota(jnp.int32, (count, count), 0)
    grid_col = lax.broadcasted_iota(jnp.int32, (count, count), 1)
    return jnp.sum(jnp.where(grid_row == grid_col, row, 0), axis=1, keepdims=True)


def home_positions(worker_row, slot_row, slots):
    same = to_column(worker_row) == worker_row
    ahead = to_column(slot_row) < slot_row
    rank = jnp.sum(jnp.where(same & ahead, 1, 0), axis=0, keepdims=True)
    return worker_row * slots + rank


def home_onehot(worker_row, slot_row, rows):
    positions = home_positions(worker_row, slot_row, ROW)
    row_ids = lax.broadcasted_iota(jnp.int32, (rows, positions.shape[1]), 0)
    return (row_ids == positions).astype(jnp.float32)


def work_positions(source_row, slots):
    count = source_row.shape[1]
    slot_ids = lax.broadcasted_iota(jnp.int32, (count, count), 0)
    later_ids = lax.broadcasted_iota(jnp.int32, (count, count), 1)
    same = to_column(source_row) == source_row
    rank = jnp.sum(jnp.where(same & (slot_ids < later_ids), 1, 0), axis=0, keepdims=True)
    shifted = jnp.where(source_row >= 0, source_row * slots + rank + 2, 0)
    grid_row = lax.broadcasted_iota(jnp.int32, (SLOT_PAD, count), 0)
    grid_col = lax.broadcasted_iota(jnp.int32, (SLOT_PAD, count), 1)
    return jnp.sum(jnp.where(grid_row == grid_col, shifted, 0), axis=1, keepdims=True) - 2


def folded_positions(row_ids, fold, tile, slots):
    inside = fold * ROW + (row_ids & (ROW - 1)) - tile * slots
    target = (row_ids >> 4) * slots + inside
    return jnp.where((inside >= 0) & (inside < slots), target, -1)


def dot_nt(left, right, **kwargs):
    return lax.dot_general(
        left, right, (((1,), (1,)), ((), ())), preferred_element_type=jnp.float32, **kwargs
    )


def dot_tn(left, right, **kwargs):
    return lax.dot_general(
        left, right, (((0,), (0,)), ((), ())), preferred_element_type=jnp.float32, **kwargs
    )


def split_wide(values):
    high = values.astype(jnp.bfloat16)
    return high, (values - high.astype(jnp.float32)).astype(jnp.bfloat16)


MESH = pl.DeviceIdType.MESH


def greet(targets):
    barrier = pltpu.get_barrier_semaphore()
    for device in targets:
        pl.semaphore_signal(barrier, inc=1, device_id=device, device_id_type=MESH)
    pl.semaphore_wait(barrier, len(targets))


def exchange(send_ref, recv_ref, send_sems, recv_sems, me, workers):
    copies = []
    for offset in range(1, workers):
        peer = lax.rem(me + offset, workers)
        source = lax.rem(me + workers - offset, workers)
        sent = pltpu.make_async_remote_copy(
            src_ref=send_ref.at[pl.ds(pl.multiple_of(peer * ROW, ROW), ROW)],
            dst_ref=recv_ref.at[pl.ds(pl.multiple_of(me * ROW, ROW), ROW)],
            send_sem=send_sems.at[peer],
            recv_sem=recv_sems.at[me],
            device_id={"rve": peer},
            device_id_type=MESH,
        )
        sent.start()
        landing = recv_ref.at[pl.ds(pl.multiple_of(source * ROW, ROW), ROW)]
        arrival = pltpu.make_async_remote_copy(
            src_ref=landing,
            dst_ref=landing,
            send_sem=send_sems.at[peer],
            recv_sem=recv_sems.at[source],
            device_id={"rve": peer},
            device_id_type=MESH,
        )
        copies.append((sent, arrival))
    here = pl.ds(pl.multiple_of(me * ROW, ROW), ROW)
    recv_ref[here, :] = send_ref[here, :]
    return copies


def step_kernel(
    strain_hbm, fiber_hbm, gradient_hbm, volume_hbm, corner_hbm, worker_hbm, slot_hbm, element_hbm,
    state_hbm, loading_hbm, compliance_hbm, new_hbm, own_ref,
    strain_ref, fiber_ref, gradient_ref, volume_ref, corner_ref, worker_ref, slot_ref, element_ref,
    state_ref, loading_ref, left_ref, lower_ref, got_ref, net_ref, send_buf,
    dense, forcing, coeff, current, pressure_a, pressure_b, back_ref, ret_ref, next_buf, prev_buf,
    load_sems, net_send, net_recv, coeff_send, coeff_recv, ret_send, ret_recv, shift_sems
):
    workers, block, width = net_ref.shape
    columns = lax.axis_size("blk")
    near = workers // 2
    piece_rows = block // (4 * PARTS)
    nodes = compliance_hbm.shape[1]
    elem_rows = fiber_hbm.shape[0]
    capacity = state_hbm.shape[1]
    rows = send_buf.shape[0]
    mean_scale = 1.0 / (3 * nodes)
    me = lax.axis_index("rve")
    lane = lax.axis_index("blk")
    z, y = me // 2, lax.rem(me, 2)
    x, core = lane // 2, lax.rem(lane, 2)
    rank = me * columns + lane
    ahead = lax.rem(rank + 1, workers * columns)
    behind = lax.rem(rank + workers * columns - 1, workers * columns)
    following = {"rve": ahead // columns, "blk": lax.rem(ahead, columns)}
    leading = {"rve": behind // columns, "blk": lax.rem(behind, columns)}
    routes = (
        {"rve": me + 2},
        {"rve": me - 2},
        {"rve": me + 1 - 2 * y},
        {"blk": lane + 2 - 4 * x},
        {"blk": lane + 1 - 2 * core},
    )
    up, down, across, over, twin = range(5)
    far = pl.multiple_of(lax.rem(me + near, workers) * block, block)
    own_slab = []
    for step in range(near):
        column = pl.multiple_of(lax.rem(me + step, workers) * block, block)
        own_slab.append((
            compliance_hbm.at[:, pl.ds(column, block)],
            net_ref.at[me, :, pl.ds(step * block, block)],
        ))
    own_slab += [
        (compliance_hbm.at[:, pl.ds(far, block // 2)], left_ref),
        (compliance_hbm.at[pl.ds(block // 2, block // 2), pl.ds(far, block)], lower_ref),
    ]
    packs = [
        (strain_hbm, strain_ref), (fiber_hbm, fiber_ref), (worker_hbm, worker_ref),
        (slot_hbm, slot_ref),
    ]
    laters = [
        (element_hbm, element_ref), (loading_hbm, loading_ref), (state_hbm, state_ref),
        (gradient_hbm, gradient_ref), (volume_hbm, volume_ref), (corner_hbm, corner_ref),
    ]
    loads = [
        pltpu.make_async_copy(src, dst, load_sems.at[at])
        for at, (src, dst) in enumerate(own_slab + packs + laters)
    ]
    for load in loads:
        load.start()
    slab_loads, pack_loads = loads[:len(own_slab)], loads[len(own_slab):len(own_slab) + len(packs)]
    later_loads = loads[len(own_slab) + len(packs):]
    greet(
        [{"rve": lax.rem(me + offset, workers)} for offset in range(1, workers)]
        + [routes[over], routes[twin], following, leading]
    )
    for load in slab_loads:
        load.wait()
    net_ref[me, :, near * block:] = jnp.where(me < near, left_ref[...], lower_ref[...].T)

    def copy(owner, q, route):
        piece = net_ref.at[owner, pl.ds(pl.multiple_of(q * piece_rows, piece_rows), piece_rows)]
        return pltpu.make_async_remote_copy(
            src_ref=piece,
            dst_ref=piece,
            send_sem=net_send.at[owner, q, route],
            recv_sem=net_recv.at[owner, q],
            device_id=routes[route],
            device_id_type=MESH,
        )

    sends = []

    def push(cond, owner, q, route):
        sends.append((cond, owner, q, route))
        if cond is True:
            copy(owner, q, route).start()
        else:
            pl.when(cond)(lambda: copy(owner, q, route).start())

    def arrive(cond, owner, q):
        if cond is True:
            copy(owner, q, twin).wait_recv()
        else:
            pl.when(cond)(lambda: copy(owner, q, twin).wait_recv())

    k, k2 = 2 * core + x, 2 * core + 1 - x
    has_up, has_down = z < near - 1, z > 0
    def parts(q):
        return [q * PARTS + part for part in range(PARTS)]

    for q in parts(k):
        push(has_up, me, q, up)
        push(has_down, me, q, down)
        push(True, me, q, across)
    for q in parts(k2):
        push(has_up, me, q, up)
        push(has_down, me, q, down)
    for load in pack_loads:
        load.wait()
    home = home_onehot(worker_ref[...], slot_ref[...], rows)
    slots_each = (capacity + workers - 1) // workers
    tiles = nodes // 128 + 1
    home_at = home_positions(worker_ref[...], slot_ref[...], slots_each)
    row_ids = lax.broadcasted_iota(jnp.int32, (rows, elem_rows), 0)
    for fold in range(send_buf.shape[1] // 128):
        packed = jnp.zeros((rows, 128), jnp.float32)
        for tile in range(fold * ROW // slots_each, (fold * ROW + ROW - 1) // slots_each + 1):
            target = folded_positions(row_ids, fold, tile, slots_each)
            picked = (target == home_at).astype(jnp.bfloat16)
            if tile < tiles - 1:
                packed += jnp.dot(
                    picked, fiber_ref[:, tile * 128:(tile + 1) * 128],
                    preferred_element_type=jnp.float32,
                )
            elif tile == tiles - 1:
                packed += jnp.concatenate(
                    [dot_nt(picked, strain_ref[...]), jnp.zeros((rows, 122), jnp.float32)], axis=1
                )
        send_buf[:, fold * 128:(fold + 1) * 128] = packed.astype(jnp.bfloat16)
    copies = exchange(send_buf, got_ref, coeff_send, coeff_recv, me, workers)

    def lines(distance):
        if distance == 0:
            return [(True, me, None, None)]
        return [
            (z >= distance, me - 2 * distance, up, has_up),
            (z < near - distance, me + 2 * distance, down, has_down),
        ]

    def from_across(distance):
        for has, owner, route, edge in lines(distance):
            other = owner + 1 - 2 * y
            for q in parts(k):
                arrive(has, other, q)
                push(has, other, q, over)
                push(has, other, q, twin)

    def from_over(distance):
        for has, owner, route, edge in lines(distance):
            other = owner + 1 - 2 * y
            for q in parts(k2):
                arrive(has, other, q)
                push(has, other, q, twin)

    def place(owner):
        rows_here = pl.ds(pl.multiple_of(owner * block, block), block)
        for step in range(near):
            there = pl.ds(pl.multiple_of(lax.rem(owner + step, workers) * block, block), block)
            tile = net_ref[owner, :, step * block:(step + 1) * block]
            dense[rows_here, there] = tile
            if step:
                dense[there, rows_here] = tile.T
        tile = net_ref[owner, :, near * block:]
        low = owner < near
        row = pl.multiple_of(jnp.where(low, owner, owner - near) * block, block)
        half = block // 2
        column = pl.multiple_of(jnp.where(low, (owner + near) * block, owner * block + half), half)
        dense[pl.ds(row, block), pl.ds(column, half)] = tile
        dense[pl.ds(column, half), pl.ds(row, block)] = tile.T

    def finish(z_other, y_other):
        owner = z_other * 2 + y_other
        for q in parts(2 - 2 * core) + parts(3 - 2 * core):
            arrive(True, owner, q)
        place(owner)

    def setup():
        for load in later_loads:
            load.wait()
        for sent, arrival in copies:
            arrival.wait_recv()
        element_row = element_ref[...]
        source = jnp.full(element_row.shape, -1, jnp.int32)
        for worker in range(workers):
            source += jnp.where(element_row >= worker * elem_rows * columns, 1, 0)
        lane_at = lax.broadcasted_iota(jnp.int32, (SLOT_PAD, rows), 1)
        onehot = (lane_at == work_positions(source, ROW)).astype(jnp.float32)
        work_at = work_positions(source, slots_each)
        for tile in range(tiles):
            wanted = jnp.zeros((SLOT_PAD, 128), jnp.float32)
            first, final = tile * slots_each // ROW, (tile * slots_each + slots_each - 1) // ROW
            for fold in range(first, final + 1):
                target = folded_positions(lane_at, fold, tile, slots_each)
                wanted += jnp.dot(
                    (target == work_at).astype(jnp.bfloat16),
                    got_ref[:, fold * 128:(fold + 1) * 128],
                    preferred_element_type=jnp.float32,
                )
            if tile < tiles - 1:
                coeff[:, tile * 128:(tile + 1) * 128] = wanted
        strain_rows = wanted[:, :8].astype(jnp.bfloat16)
        forcing[0:LOAD_PAD, :] = jnp.zeros((LOAD_PAD, nodes), jnp.float32)
        for k_load in range(6):
            three = loading_ref[k_load].astype(jnp.float32)
            for axis in range(3):
                forcing[axis * 8 + k_load:axis * 8 + k_load + 1, :] = three[axis:axis + 1, :]
        current[0:LOAD_PAD, :] = jnp.zeros((LOAD_PAD, nodes), jnp.float32)
        for axis in range(3):
            start = LOAD_PAD + axis * SLOT_PAD
            load_rows = forcing[axis * 8:axis * 8 + 8, :].astype(jnp.bfloat16)
            forcing[start:start + SLOT_PAD, :] = jnp.dot(
                strain_rows, load_rows, preferred_element_type=jnp.float32
            )
            current[start + 80:start + SLOT_PAD, :] = jnp.zeros((SLOT_PAD - 80, nodes), jnp.float32)
            current[start:start + capacity, :] = state_ref[axis]
        for tile in range(nodes // block):
            lanes = slice(tile * block, (tile + 1) * block)
            pressure_a[:, lanes] = press(current[:, lanes], lanes)
        return onehot

    def press(values, lanes):
        c = coeff[:, lanes]
        wide = jnp.concatenate([jnp.zeros((LOAD_PAD, c.shape[1]), jnp.float32), c, c, c], axis=0)
        return (forcing[:, lanes] - wide * jnp.tanh(values)).astype(jnp.bfloat16)

    last = near - 1
    full = 1
    z_one = z + 1 - 2 * lax.rem(z, 2)
    z_two = lax.rem(z + 2, near)
    z_three = last - z

    def from_over_line(distance):
        for has, owner, route, edge in lines(distance):
            for q in parts(k2):
                arrive(has, owner, q)
                push(has, owner, q, twin)

    from_across(0)
    for distance in range(1, near):
        for has, owner, route, edge in lines(distance):
            for q in parts(k):
                arrive(has, owner, q)
                if distance < last:
                    push(has & edge, owner, q, route)
                push(has, owner, q, across)
                if distance > full:
                    push(has, owner, q, over)
                push(has, owner, q, twin)
        if distance <= full:
            for has, owner, route, edge in lines(distance):
                for q in parts(k2):
                    arrive(has, owner, q)
                    if distance + 1 <= full:
                        push(has & edge, owner, q, route)
                    push(has, owner, q, twin)
        from_over(distance - 1)
        if distance - 1 > full:
            from_over_line(distance - 1)
        from_across(distance)
        if distance == 2:
            place(me)
            finish(z, 1 - y)
    onehot = setup()
    finish(z_one, y)
    from_over_line(last)
    finish(z_one, 1 - y)
    finish(z_two, y)
    from_over(last)
    finish(z_three, y)
    finish(z_two, 1 - y)
    finish(z_three, 1 - y)

    for iteration in range(ITERS):
        reads, writes = (pressure_a, pressure_b) if iteration % 2 == 0 else (pressure_b, pressure_a)
        for tile in range(nodes // block):
            lanes = slice(tile * block, (tile + 1) * block)
            values = jnp.dot(reads[...], dense[:, lanes], preferred_element_type=jnp.float32)
            if iteration == ITERS - 1:
                current[:, lanes] = values
            else:
                writes[:, lanes] = press(values, lanes)

    occupied = jnp.sum(onehot, axis=1, keepdims=True) > 0.5
    tangent = jnp.zeros((SLOT_PAD, 96), jnp.float32)
    tangent_low = jnp.zeros((SLOT_PAD, 48), jnp.float32)
    stress = jnp.zeros((SLOT_PAD, 8), jnp.float32)
    fixed = jnp.zeros((8, 8), jnp.float32)
    for axis in range(3):
        start = LOAD_PAD + axis * SLOT_PAD
        final = current[start:start + SLOT_PAD, :]
        state_ref[axis] = jnp.where(
            occupied[:capacity], current[start:start + capacity, :], state_ref[axis]
        )
        basis = current[axis * 8:axis * 8 + 8, :]
        load = forcing[axis * 8:axis * 8 + 8, :].astype(jnp.bfloat16)
        products = jnp.concatenate([basis[k:k + 1, :] * basis for k in range(6)], axis=0)
        products_high, products_low = split_wide(products)
        damping = coeff[...] * (1.0 - jnp.tanh(final) ** 2)
        damping_high, damping_low = split_wide(damping)
        tangent += dot_nt(damping_high, jnp.concatenate([products_high, products_low], axis=0))
        tangent_low += dot_nt(damping_low, products_high)
        final_high, final_low = split_wide(final)
        stress += dot_nt(final_high, load) + dot_nt(final_low, load)
        basis_high, basis_low = split_wide(basis)
        fixed += dot_nt(load, basis_high) + dot_nt(load, basis_low)
    store = pltpu.make_async_copy(state_ref, new_hbm, load_sems.at[len(loads)])
    store.start()
    lane_ids = lax.broadcasted_iota(jnp.int32, (8, 48), 1)
    row_ids = lax.broadcasted_iota(jnp.int32, (8, 48), 0)
    spread = jnp.dot(
        fixed, (lane_ids % 8 == row_ids).astype(jnp.float32), precision=highest,
        preferred_element_type=jnp.float32,
    )
    fixed_row = jnp.sum(jnp.where(lane_ids // 8 == row_ids, spread, 0.0), axis=0, keepdims=True)
    total = fixed_row - (tangent[:, :48] + tangent[:, 48:] + tangent_low)
    packed = jnp.concatenate(
        [total, stress, jnp.zeros((SLOT_PAD, 72), jnp.float32)], axis=1
    ) * mean_scale
    back_ref[...] = dot_tn(onehot, packed, precision=highest)
    returns = exchange(back_ref, ret_ref, ret_send, ret_recv, me, workers)
    for sent, arrival in copies:
        sent.wait_send()
    for cond, owner, q, route in sends:
        if cond is True:
            copy(owner, q, route).wait_send()
        else:
            pl.when(cond)(lambda: copy(owner, q, route).wait_send())
    for sent, arrival in returns:
        arrival.wait_recv()
    values = dot_tn(ret_ref[...], home, precision=highest)
    volume = volume_ref[...]
    count = volume.shape[1]
    stress = [values[48 + k:49 + k, :] for k in range(6)]
    rows_of = [values[k * 8:k * 8 + 8, :] for k in range(6)]
    node_ids = lax.broadcasted_iota(jnp.int32, (2 * NODE_DEV, count), 0)
    assembled = jnp.zeros((16, 2 * NODE_DEV), jnp.float32)

    def apply(g, terms):
        gx, gy, gz = g
        return (
            gx * terms[0] + gz * terms[4] + gy * terms[5],
            gy * terms[1] + gz * terms[3] + gx * terms[5],
            gz * terms[2] + gy * terms[3] + gx * terms[4],
        )

    for corner in range(4):
        g = [gradient_ref[3 * corner + c:3 * corner + c + 1, :] for c in range(3)]
        lines = [volume * f for f in apply(g, stress)]
        for u in apply(g, rows_of):
            lines += [volume * m for m in apply(g, [u[j:j + 1, :] for j in range(6)])]
        contrib = jnp.concatenate(lines + [jnp.zeros((4, count), jnp.float32)], axis=0)
        picked = (node_ids == corner_ref[corner:corner + 1, :] - rank * NODE_DEV).astype(jnp.float32)
        assembled += dot_nt(contrib, picked, precision=highest)
    next_buf[...] = assembled[:, NODE_DEV:]
    shift = pltpu.make_async_remote_copy(
        src_ref=next_buf, dst_ref=prev_buf, send_sem=shift_sems.at[0], recv_sem=shift_sems.at[1],
        device_id=following, device_id_type=MESH,
    )
    shift.start()
    for sent, arrival in returns:
        sent.wait_send()
    shift.wait()
    own_ref[...] = assembled[:, :NODE_DEV] + jnp.where(rank > 0, prev_buf[...], 0.0)
    store.wait()


def deliver_kernel(solved_hbm, own_ref, new_hbm, force_ref, block_ref, held, in_sems, out_sems):
    width = solved_hbm.shape[2] // 4
    chunks = [(axis, cut) for axis in range(3) for cut in range(4)]

    def part(ref, axis, cut):
        return ref.at[axis, :, pl.ds(cut * width, width)]

    arriving = [
        pltpu.make_async_copy(part(solved_hbm, *at), part(held, *at), in_sems.at[at])
        for at in chunks
    ]
    leaving = [
        pltpu.make_async_copy(part(held, *at), part(new_hbm, *at), out_sems.at[at])
        for at in chunks
    ]
    for copy in arriving:
        copy.start()
    force_ref[...] = own_ref[0:3, :]
    block_ref[...] = own_ref[3:12, :]
    for came, goes in zip(arriving, leaving):
        came.wait()
        goes.start()
    for copy in leaving:
        copy.wait()


def tiled_body(
    strain, fiber_coeff, gradients, volume, corners, rve_worker, rve_slot, slot_element,
    state_table, loading, compliance,
):
    elem_rows = strain.shape[0]
    workers = lax.axis_size("rve")
    capacity = state_table.shape[0]
    nodes = compliance.shape[1]
    block = compliance.shape[0]
    rows = workers * ROW
    total = LOAD_PAD + 3 * SLOT_PAD
    slots_each = (capacity + workers - 1) // workers
    folded = ((nodes // 128 + 1) * slots_each + ROW - 1) // ROW
    vmem = pl.BlockSpec(memory_space=pltpu.VMEM)
    hbm = pl.BlockSpec(memory_space=pl.ANY)
    wide, narrow, whole = jnp.float32, jnp.bfloat16, jnp.int32
    dma = pltpu.SemaphoreType.DMA
    solved, own_rows = pl.pallas_call(
        step_kernel,
        out_shape=(
            jax.ShapeDtypeStruct((3, capacity, nodes), wide),
            jax.ShapeDtypeStruct((16, NODE_DEV), wide),
        ),
        in_specs=[hbm] * 11, out_specs=(hbm, vmem),
        scratch_shapes=[
            pltpu.VMEM((6, elem_rows), narrow),
            pltpu.VMEM((elem_rows, nodes), narrow),
            pltpu.VMEM((12, elem_rows), wide),
            pltpu.VMEM((1, elem_rows), wide),
            pltpu.VMEM((4, elem_rows), whole),
            pltpu.VMEM((1, elem_rows), whole),
            pltpu.VMEM((1, elem_rows), whole),
            pltpu.VMEM((1, capacity), whole),
            pltpu.VMEM((3, capacity, nodes), wide),
            pltpu.VMEM((6, 3, nodes), narrow),
            pltpu.VMEM((block, block // 2), narrow),
            pltpu.VMEM((block // 2, block), narrow),
            pltpu.VMEM((rows, folded * 128), narrow),
            pltpu.VMEM((workers, block, workers // 2 * block + block // 2), narrow),
            pltpu.VMEM((rows, folded * 128), narrow),
            pltpu.VMEM((nodes, nodes), narrow),
            pltpu.VMEM((total, nodes), wide),
            pltpu.VMEM((SLOT_PAD, nodes), wide),
            pltpu.VMEM((total, nodes), wide),
            pltpu.VMEM((total, nodes), narrow),
            pltpu.VMEM((total, nodes), narrow),
            pltpu.VMEM((rows, 128), wide),
            pltpu.VMEM((rows, 128), wide),
            pltpu.VMEM((16, NODE_DEV), wide),
            pltpu.VMEM((16, NODE_DEV), wide),
            dma((workers // 2 + 13,)),
            dma((workers, 4 * PARTS, 5)),
            dma((workers, 4 * PARTS)),
            dma((workers,)),
            dma((workers,)),
            dma((workers,)),
            dma((workers,)),
            dma((2,)),
        ],
        compiler_params=pltpu.CompilerParams(
            vmem_limit_bytes=58 * 2**20, collective_id=0, has_side_effects=True
        ),
        name="step",
    )(
        strain.T, fiber_coeff, gradients, volume[None, :], corners, rve_worker[None, :],
        rve_slot[None, :], slot_element[None, :], jnp.transpose(state_table, (1, 0, 2)),
        loading, compliance,
    )
    new_table, forces, blocks = pl.pallas_call(
        deliver_kernel,
        out_shape=(
            jax.ShapeDtypeStruct((3, capacity, nodes), wide),
            jax.ShapeDtypeStruct((3, NODE_DEV), wide),
            jax.ShapeDtypeStruct((9, NODE_DEV), wide),
        ),
        in_specs=[hbm, vmem], out_specs=(hbm, vmem, vmem),
        scratch_shapes=[pltpu.VMEM((3, capacity, nodes), wide), dma((3, 4)), dma((3, 4))],
        compiler_params=pltpu.CompilerParams(vmem_limit_bytes=58 * 2**20),
        name="deliver",
    )(solved, own_rows)
    return jnp.transpose(new_table, (1, 0, 2)), forces, blocks


def solution(mesh):
    def chosen(*args):
        workers, columns = lax.axis_size("rve"), lax.axis_size("blk")
        block = args[-1].shape[0]
        even = workers == 8 and columns == 4 and block % 256 == 0
        few = -(-args[8].shape[0] // workers) <= ROW and args[8].shape[0] <= SLOT_PAD
        return (tiled_body if even and few else body)(*args)

    return jax.shard_map(
        chosen,
        mesh=mesh,
        in_specs=(
            P(("rve", "blk"), None),
            P(("rve", "blk"), None),
            P(None, ("rve", "blk")),
            P(("rve", "blk")),
            P(None, ("rve", "blk")),
            P(("rve", "blk")),
            P(("rve", "blk")),
            P(("rve", "blk")),
            P(("rve", "blk"), None, None),
            P(),
            P("rve", None),
        ),
        out_specs=(P(("rve", "blk"), None, None), P(None, ("rve", "blk")), P(None, ("rve", "blk"))),
        check_vma=False,
    )
```
